32 devices in a mesh: comp: 8 (over y, x, core), band: 4 (over z).
Axes of the slice: x: 2, y: 2, z: 4, core: 2. Of those that a mesh axis runs over, the one named last changes fastest.
Arguments:
- spectrum: float32 [1152, 96, 256], P('comp', 'band'), as said below
- wet_mask: int32 [96, 256], P('band'), may hold values 0 or 1
- quad_matrix: bfloat16 [1152, 1152], replicated, may hold values from -0.1875 to 0.1875
- dissipation: float32 [1152], replicated, may hold values from 0.2 to 2
- circulation: float32 [3, 32, 1024], P(None, 'band', 'comp'), may hold values from -3 to 3
- source_points: int32 [3, 32, 1024], P(None, 'band', 'comp'), may hold values from 0 to 6143
Outputs:
- spectrum_out: float32 [1152, 96, 256], P('comp', 'band')
- circulation_out: float32 [3, 32, 1024], P(None, 'band', 'comp')
The draws below stay inside these ranges and needn't reach their ends.
Inputs may be any that keep to these rules, and one draw needn't show every extreme that they name: `spectrum`: every entry is positive. `source_points`: each entry numbers a wave point of the band that holds the cell's row, row by row within the band.
All inputs are finite; a program needn't handle non-finite values. No bound on the sum of `wet_mask` on one device may be relied on, other than what follows from the above.
Results may differ from the reference program's by a relative error of at most 0.007.
Values may be sent and summed in bfloat16 or wider, within the bound.
A program may use at most 128 MiB of HBM per device.

```python
import math
import jax
import jax.numpy as jnp
from jax import lax

NF = 36
ND = 32
K = 1152
NY = 256
NX = 96
BAND_PTS = 6144
SUBSTEPS = 4
SRC_STEPS = 4
SW_STEPS = 8
TILE_X = 8
MX = 32
MY = 1024


def draw_spectrum(key, part):
    key_comp, key_point, key_jitter = jax.random.split(jax.random.fold_in(key, 11), 3)
    comp_low, comp_high, point_low, point_high, jitter_low, jitter_high = (0.3, 3.0, 0.5, 2.0, 0.5, 1.5)
    comp_scale = jnp.exp(jax.random.uniform(key_comp, (NF * ND, 1, 1), jnp.float32, math.log(comp_low), math.log(comp_high)))
    point_scale = jnp.exp(jax.random.uniform(key_point, (1, NX, NY), jnp.float32, math.log(point_low), math.log(point_high)))
    jitter = jax.random.uniform(key_jitter, (NF * ND, NX, NY), jnp.float32, jitter_low, jitter_high)
    return comp_scale * point_scale * jitter


def set_ends(array, stream_key, smallest, largest):
    spot = [jax.random.randint(jax.random.fold_in(stream_key, axis), (), 0, length) for axis, length in enumerate(array.shape)]
    longest = array.shape.index(max(array.shape))
    next_to = spot[:longest] + [(spot[longest] + 1) % array.shape[longest]] + spot[longest + 1:]
    return array.at[tuple(spot)].set(smallest).at[tuple(next_to)].set(largest)


def level_of(stream_key, extent, cuts, smallest, top_value):
    level, own = 1.0, jax.random.fold_in(stream_key, 6)
    for dim, blocks in cuts:
        heights = jnp.exp(jax.random.uniform(jax.random.fold_in(own, dim), (blocks,), jnp.float32, smallest / len(cuts), top_value / len(cuts)))
        level = level * jnp.repeat(heights, extent[dim] // blocks).reshape([-1 if axis == dim else 1 for axis in range(len(extent))])
    return level


def gaussian(stream_key, extent, scale, limit, cuts=(), kind=jnp.bfloat16):
    drawn = scale * jax.random.normal(stream_key, extent, jnp.float32)
    if cuts:
        drawn = drawn * level_of(stream_key, extent, cuts, -0.22, 0.18)
    return jnp.clip(drawn, -limit, limit).astype(kind)


def setup_inputs(seed: int = 0) -> dict:
    key_of = jax.random.split(jax.random.key(seed), 7)
    spectrum = draw_spectrum(jax.random.fold_in(key_of[6], 71), 0)
    wet_mask = set_ends((jax.random.randint(key_of[1], (NX, NY), 0, 8) < 7).astype(jnp.int32), jax.random.fold_in(key_of[1], 1), 0, 1)
    quad_matrix = gaussian(key_of[2], (K, K), K ** -0.5, 0.1875)
    dissipation = jnp.clip(jnp.exp(jax.random.uniform(key_of[3], (K,), jnp.float32, math.log(0.2), math.log(2.0))), 0.2, 2.0)
    circulation = gaussian(key_of[4], (3, MX, MY), 0.5, 3.0, ((1, 4), (2, 8)), jnp.float32)
    source_points = set_ends(jax.random.randint(key_of[5], (3, MX, MY), 0, BAND_PTS), jax.random.fold_in(key_of[5], 1), 0, BAND_PTS - 1).astype(jnp.int32)
    return {"spectrum": spectrum, "wet_mask": wet_mask, "quad_matrix": quad_matrix, "dissipation": dissipation, "circulation": circulation, "source_points": source_points}


step_source = 0.1
wave_speed = 0.35
friction = 0.05
forcing_gain = 0.15


def component_tables(offset, local_count, freqs, headings):
    indices = offset + jnp.arange(local_count, dtype=jnp.int32)
    frequency = (indices // headings).astype(jnp.float32)
    heading = (indices % headings).astype(jnp.float32)
    heading_angle = 2.0 * math.pi * (heading + 0.5) / headings
    fraction = (frequency + 0.5) / freqs
    group_speed = 0.25 + 0.4 * fraction
    wave_ratio = 0.5 + 0.5 * fraction
    cosine = jnp.cos(heading_angle)
    sine_part = jnp.sin(heading_angle)
    speed_east = group_speed * cosine
    speed_north = group_speed * sine_part
    stress_coef = jnp.stack([wave_ratio * (1.0 + cosine * cosine) - 0.5,
                             wave_ratio * sine_part * cosine,
                             wave_ratio * (1.0 + sine_part * sine_part) - 0.5])
    return speed_east, speed_north, stress_coef


def upwind(extended, speed_east, speed_north, wet_rows):
    middle = extended[:, 1:-1, :]
    west_cells = extended[:, :-2, :]
    east_cells = extended[:, 2:, :]
    padded = jnp.pad(middle, ((0, 0), (0, 0), (1, 1)))
    south_cells = padded[:, :, :-2]
    north_cells = padded[:, :, 2:]
    along_rows = speed_east[:, None, None]
    along_cols = speed_north[:, None, None]
    flux_rows = jnp.maximum(along_rows, 0.0) * (middle - west_cells) + jnp.minimum(along_rows, 0.0) * (east_cells - middle)
    flux_cols = jnp.maximum(along_cols, 0.0) * (middle - south_cells) + jnp.minimum(along_cols, 0.0) * (north_cells - middle)
    return (middle - flux_rows - flux_cols) * wet_rows


def rounded(values):
    return lax.optimization_barrier(values.astype(jnp.bfloat16)).astype(jnp.float32)


def sources(base, quad_matrix, dissipation):
    current = base
    for repeat in range(SRC_STEPS):
        product = jnp.dot(quad_matrix, current.astype(jnp.bfloat16), preferred_element_type=jnp.float32)
        energy_level = jnp.mean(current, axis=0, keepdims=True)
        current = current + step_source * current * (product - dissipation[:, None] * energy_level)
    return current


def diff_rows(extended):
    return 0.5 * (extended[2:, 1:-1] - extended[:-2, 1:-1])


def diff_cols(extended):
    return 0.5 * (extended[1:-1, 2:] - extended[1:-1, :-2])


def reference(spectrum, wet_mask, quad_matrix, dissipation, circulation, source_points):
    component_total = NF * ND
    speed_east, speed_north, stress_coef = component_tables(0, component_total, NF, ND)
    wetness = wet_mask.astype(jnp.float32)[None]
    per_frequency = spectrum.reshape(NF, ND, NX, NY)

    def propagate(packed):
        slab_block, east_part, north_part = packed
        for substep in range(SUBSTEPS):
            extended = jnp.pad(slab_block, ((0, 0), (1, 1), (0, 0)))
            slab_block = upwind(extended, east_part, north_part, wetness)
        return slab_block

    propagated = lax.map(propagate, (per_frequency, speed_east.reshape(NF, ND), speed_north.reshape(NF, ND)))
    propagated = propagated.reshape(component_total, NX, NY)
    per_row = jnp.moveaxis(propagated, 1, 0)

    def row_work(slab_row):
        base = rounded(slab_row)
        current = sources(base, quad_matrix, dissipation)
        increment = rounded(current - base)
        coupled = base + increment
        stress = jnp.dot(stress_coef, coupled, precision=lax.Precision.HIGHEST) / component_total
        return slab_row + increment, stress

    finished, row_stress = lax.map(row_work, per_row)
    new_spectrum = jnp.moveaxis(finished, 0, 1)
    stress_flat = jnp.moveaxis(row_stress, 0, 1).reshape(3, NX * NY)
    band_offset = (jnp.arange(MX, dtype=jnp.int32) // TILE_X) * BAND_PTS
    global_index = source_points + band_offset[None, :, None]
    picked = jnp.take(stress_flat, global_index.reshape(-1), axis=1).reshape(3, 3, MX, MY)
    cell_stress = 0.5 * picked[:, 0] + 0.3 * picked[:, 1] + 0.2 * picked[:, 2]
    rimmed = jnp.pad(cell_stress, ((0, 0), (1, 1), (1, 1)))
    force_down = -(diff_rows(rimmed[0]) + diff_cols(rimmed[1]))
    force_across = -(diff_rows(rimmed[1]) + diff_cols(rimmed[2]))
    height = circulation[0]
    flow_down = circulation[1]
    flow_across = circulation[2]
    for repeat in range(SW_STEPS):
        down_ext = jnp.pad(flow_down, 1)
        across_ext = jnp.pad(flow_across, 1)
        height = height - wave_speed * (diff_rows(down_ext) + diff_cols(across_ext))
        height_ext = jnp.pad(height, 1)
        flow_down = (1.0 - friction) * flow_down - wave_speed * diff_rows(height_ext) + forcing_gain * force_down
        flow_across = (1.0 - friction) * flow_across - wave_speed * diff_cols(height_ext) + forcing_gain * force_across
    return new_spectrum, jnp.stack([height, flow_down, flow_across])
```

```python
import functools
import math

import jax
import jax.numpy as jnp
from jax import lax
from jax.experimental import pallas as pl
from jax.experimental.pallas import tpu as pltpu
from jax.sharding import PartitionSpec as P

NF = 36
ND = 32
SUBSTEPS = 4
SRC_STEPS = 4
SW_STEPS = 8
COMP_BLOCK = 16
LANES = 128
VMEM_LIMIT = 50 * 1024 * 1024

step_source = 0.1
wave_speed = 0.35
friction = 0.05
forcing_gain = 0.15


def neighbours(cells, axis, dim, width):
    count = lax.axis_size(axis)
    ends = count - 1
    head = lax.slice_in_dim(cells, 0, width, axis=dim)
    tail = lax.slice_in_dim(cells, cells.shape[dim] - width, cells.shape[dim], axis=dim)
    before = lax.ppermute(tail, axis, [(i, i + 1) for i in range(ends)])
    after = lax.ppermute(head, axis, [(i + 1, i) for i in range(ends)])
    return before, after


def component_tables(offset, local_count, freqs, headings):
    indices = offset + jnp.arange(local_count, dtype=jnp.int32)
    frequency = (indices // headings).astype(jnp.float32)
    heading = (indices % headings).astype(jnp.float32)
    heading_angle = 2.0 * math.pi * (heading + 0.5) / headings
    fraction = (frequency + 0.5) / freqs
    group_speed = 0.25 + 0.4 * fraction
    wave_ratio = 0.5 + 0.5 * fraction
    cosine = jnp.cos(heading_angle)
    sine_part = jnp.sin(heading_angle)
    stress_coef = jnp.stack(
        [
            wave_ratio * (1.0 + cosine * cosine) - 0.5,
            wave_ratio * sine_part * cosine,
            wave_ratio * (1.0 + sine_part * sine_part) - 0.5,
        ]
    )
    return (group_speed * cosine, group_speed * sine_part, stress_coef)


def propagate_kernel(rows, *refs):
    x_refs = refs[:-6]
    before_ref, after_ref, wet_ref, speed_ref, dens_ref, sent_ref = refs[-6:]
    columns = dens_ref.shape[2]
    lane = lax.broadcasted_iota(jnp.int32, (8, columns), 1)
    before = before_ref[...].astype(jnp.float32)
    after = after_ref[...].astype(jnp.float32)
    total = rows + 2 * SUBSTEPS
    for half in range(COMP_BLOCK // 8):
        c0 = half * 8
        ax = jnp.broadcast_to(speed_ref[c0 : c0 + 8, 0:1], (8, columns))
        ay = jnp.broadcast_to(speed_ref[c0 : c0 + 8, 1:2], (8, columns))
        keep = 1.0 - jnp.abs(ax) - jnp.abs(ay)
        west, east = jnp.maximum(ax, 0.0), jnp.maximum(-ax, 0.0)
        south = jnp.where(lane > 0, jnp.maximum(ay, 0.0), 0.0)
        north = jnp.where(lane < columns - 1, jnp.maximum(-ay, 0.0), 0.0)
        stages = [dict() for _ in range(SUBSTEPS + 1)]
        for r in range(total):
            if r < SUBSTEPS:
                stages[0][r] = before[r, c0 : c0 + 8]
            elif r < SUBSTEPS + rows:
                part = pl.ds(c0 * rows + r - SUBSTEPS, 8, stride=rows)
                stages[0][r] = jnp.concatenate([x_ref[part, :] for x_ref in x_refs], axis=1)
            else:
                stages[0][r] = after[r - SUBSTEPS - rows, c0 : c0 + 8]
            for s in range(1, SUBSTEPS + 1):
                q = r - s
                if q < s or q >= total - s:
                    continue
                old = stages[s - 1]
                middle = old[q]
                value = (
                    keep * middle
                    + west * old[q - 1]
                    + east * old[q + 1]
                    + south * pltpu.roll(middle, 1, 1)
                    + north * pltpu.roll(middle, columns - 1, 1)
                ) * wet_ref[q : q + 1, :]
                stages[s][q] = value
                if s == SUBSTEPS:
                    dens_ref[q - SUBSTEPS, c0 : c0 + 8, :] = value
    sent_ref[...] = dens_ref[...].astype(jnp.bfloat16)


def propagate(spectrum, before, after, wet, speeds):
    count, rows, columns = spectrum.shape
    grid = (pl.cdiv(count, COMP_BLOCK),)
    parts = columns // LANES
    flat = spectrum.reshape(count * rows, columns)
    return pl.pallas_call(
        functools.partial(propagate_kernel, rows),
        grid=grid,
        in_specs=[
            pl.BlockSpec((COMP_BLOCK * rows, LANES), functools.partial(lambda p, i: (i, p), p))
            for p in range(parts)
        ]
        + [
            pl.BlockSpec((SUBSTEPS, COMP_BLOCK, columns), lambda i: (0, i, 0)),
            pl.BlockSpec((SUBSTEPS, COMP_BLOCK, columns), lambda i: (0, i, 0)),
            pl.BlockSpec((rows + 2 * SUBSTEPS, columns), lambda i: (0, 0)),
            pl.BlockSpec((COMP_BLOCK, 2), lambda i: (i, 0)),
        ],
        out_specs=[
            pl.BlockSpec((rows, COMP_BLOCK, columns), lambda i: (0, i, 0)),
            pl.BlockSpec((rows, COMP_BLOCK, columns), lambda i: (0, i, 0)),
        ],
        out_shape=[
            jax.ShapeDtypeStruct((rows, count, columns), jnp.float32),
            jax.ShapeDtypeStruct((rows, count, columns), jnp.bfloat16),
        ],
        compiler_params=pltpu.CompilerParams(vmem_limit_bytes=VMEM_LIMIT),
    )(*[flat] * parts, before, after, wet, speeds)


def finish_kernel(rows, dens_ref, inc_ref, out_ref, *parts):
    for r in range(rows):
        value = dens_ref[r] + inc_ref[r].astype(jnp.float32)
        for c0 in range(0, COMP_BLOCK, 8):
            for p, part in enumerate(parts):
                part[pl.ds(c0 * rows + r, 8, stride=rows), :] = value[
                    c0 : c0 + 8, p * LANES : (p + 1) * LANES
                ]
    for p, part in enumerate(parts):
        out_ref[:, p * LANES : (p + 1) * LANES] = part[...]


def finish(density, increment):
    rows, count, columns = density.shape
    spec = pl.BlockSpec((rows, COMP_BLOCK, columns), lambda i: (0, i, 0))
    out = pl.pallas_call(
        functools.partial(finish_kernel, rows),
        grid=(pl.cdiv(count, COMP_BLOCK),),
        in_specs=[spec, spec],
        out_specs=pl.BlockSpec((COMP_BLOCK * rows, columns), lambda i: (i, 0)),
        out_shape=jax.ShapeDtypeStruct((count * rows, columns), jnp.float32),
        scratch_shapes=[pltpu.VMEM((COMP_BLOCK * rows, LANES), jnp.float32)] * (columns // LANES),
        compiler_params=pltpu.CompilerParams(vmem_limit_bytes=VMEM_LIMIT),
    )(density, increment)
    return out.reshape(count, rows, columns)


def row_sources(base_ref, quad_ref, diss_ref, coef_ref, cur, low, inc_ref):
    blocks, count, columns = base_ref.shape
    total = blocks * count
    tiles = 3
    tile = total // tiles
    base = base_ref[...].reshape(total, columns)
    low[0] = base
    cur[...] = base.astype(jnp.float32)
    level = jnp.sum(cur[...], axis=0, keepdims=True)
    for s in range(SRC_STEPS):
        after = jnp.zeros_like(level)
        for t in range(tiles):
            part = slice(t * tile, (t + 1) * tile)
            product = jnp.dot(quad_ref[part, :], low[s % 2], preferred_element_type=jnp.float32)
            now = cur[part, :]
            now = now + step_source * now * (product - diss_ref[part, :] * (level / total))
            cur[part, :] = now
            after = after + jnp.sum(now, axis=0, keepdims=True)
            if s < SRC_STEPS - 1:
                low[(s + 1) % 2, part, :] = now.astype(jnp.bfloat16)
        level = after
    wide = base_ref[...].reshape(total, columns).astype(jnp.float32)
    increment = (cur[...] - wide).astype(jnp.bfloat16)
    inc_ref[...] = increment.reshape(blocks, count, columns)
    coupled = wide + increment.astype(jnp.float32)
    return (
        jnp.dot(
            coef_ref[...],
            coupled,
            precision=lax.Precision.HIGHEST,
            preferred_element_type=jnp.float32,
        )
        / total
    )


def sources_kernel(base_ref, quad_ref, diss_ref, coef_ref, inc_ref, stress_ref, cur, low):
    stress_ref[0] = row_sources(
        base_ref.at[:, 0], quad_ref, diss_ref, coef_ref, cur, low, inc_ref.at[:, 0]
    )


def sources(base, quad_matrix, dissipation, coef):
    blocks, rows, count, columns = base.shape
    total = blocks * count
    return pl.pallas_call(
        sources_kernel,
        grid=(rows,),
        in_specs=[
            pl.BlockSpec((blocks, 1, count, columns), lambda i: (0, i, 0, 0)),
            pl.BlockSpec((total, total), lambda i: (0, 0)),
            pl.BlockSpec((total, 1), lambda i: (0, 0)),
            pl.BlockSpec(coef.shape, lambda i: (0, 0)),
        ],
        out_specs=[
            pl.BlockSpec((blocks, 1, count, columns), lambda i: (0, i, 0, 0)),
            pl.BlockSpec((1, coef.shape[0], columns), lambda i: (i, 0, 0)),
        ],
        out_shape=[
            jax.ShapeDtypeStruct(base.shape, jnp.bfloat16),
            jax.ShapeDtypeStruct((rows, coef.shape[0], columns), jnp.float32),
        ],
        scratch_shapes=[
            pltpu.VMEM((total, columns), jnp.float32),
            pltpu.VMEM((2, total, columns), jnp.bfloat16),
        ],
        compiler_params=pltpu.CompilerParams(vmem_limit_bytes=VMEM_LIMIT),
    )(base, quad_matrix, dissipation, coef)


def pick_kernel(table_ref, index_ref, out_ref):
    high = table_ref.shape[2]
    cells = index_ref.shape[2]
    table = table_ref[0].reshape(3 * high, LANES)
    result = [jnp.zeros((1, cells), jnp.float32) for _ in range(3)]
    for m, weight in enumerate((0.5, 0.3, 0.2)):
        index = index_ref[0, m : m + 1, :]
        low = index % LANES
        top = index // LANES
        lane_hit = lax.broadcasted_iota(jnp.int32, (LANES, cells), 0) == low
        ones = jnp.where(lane_hit, 1.0, 0.0).astype(jnp.bfloat16)
        spread = jnp.dot(table, ones, preferred_element_type=jnp.float32)
        row_hit = lax.broadcasted_iota(jnp.int32, (high, cells), 0) == top
        for k in range(3):
            part = jnp.where(row_hit, spread[k * high : (k + 1) * high], 0.0)
            result[k] = result[k] + weight * jnp.sum(part, axis=0, keepdims=True)
    out_ref[0] = jnp.concatenate(result, axis=0)


def pick(table, index):
    bands, _, high, _ = table.shape
    cells = index.shape[2]
    return pl.pallas_call(
        pick_kernel,
        grid=(bands,),
        in_specs=[
            pl.BlockSpec((1, 3, high, LANES), lambda b: (b, 0, 0, 0)),
            pl.BlockSpec((1, 3, cells), lambda b: (b, 0, 0)),
        ],
        out_specs=pl.BlockSpec((1, 3, cells), lambda b: (b, 0, 0)),
        out_shape=jax.ShapeDtypeStruct((bands, 3, cells), jnp.float32),
        compiler_params=pltpu.CompilerParams(vmem_limit_bytes=VMEM_LIMIT),
    )(table, index)


def diff_rows(extended):
    return 0.5 * (extended[2:, 1:-1] - extended[:-2, 1:-1])


def diff_cols(extended):
    return 0.5 * (extended[1:-1, 2:] - extended[1:-1, :-2])


def exchange_sources(sent, quad_matrix, dissipation, coef, groups):
    rows, count, columns = sent.shape
    own = rows // groups
    arrived = lax.all_to_all(sent, "comp", split_axis=0, concat_axis=0, tiled=True)
    base = arrived.reshape(groups, own, count, columns)
    if count % 16:
        base = base.transpose(1, 0, 2, 3).reshape(1, own, groups * count, columns)
    increment, stress = sources(base, quad_matrix, dissipation[:, None], coef)
    if count % 16:
        increment = increment.reshape(own, groups, count, columns).transpose(1, 0, 2, 3)
    returned = lax.all_to_all(
        increment.reshape(rows, count, columns), "comp", split_axis=0, concat_axis=0, tiled=True
    )
    return returned, stress


def on_device(spectrum, wet_mask, quad_matrix, dissipation, circulation, source_points):
    local_count, row_count, columns = spectrum.shape
    groups = lax.axis_size("comp")
    bands = lax.axis_size("band")
    own_rows = row_count // groups
    offset = lax.axis_index("comp") * local_count
    speed_x, speed_y, _ = component_tables(offset, local_count, NF, ND)
    stress_coef = component_tables(0, local_count * groups, NF, ND)[2]
    coef = jnp.pad(stress_coef, ((0, 5), (0, 0)))

    head = spectrum[:, :SUBSTEPS].transpose(1, 0, 2).astype(jnp.bfloat16)
    tail = spectrum[:, row_count - SUBSTEPS :].transpose(1, 0, 2).astype(jnp.bfloat16)
    before, after = neighbours(jnp.concatenate([head, tail], axis=0), "band", 0, SUBSTEPS)
    wet = wet_mask.astype(jnp.float32)
    wet_before, wet_after = neighbours(wet, "band", 0, SUBSTEPS)
    wet = jnp.concatenate([wet_before, wet, wet_after], axis=0)
    density, sent = propagate(
        spectrum, before, after, wet, jnp.stack([speed_x, speed_y], axis=1)
    )

    tile_rows = circulation.shape[1]
    tile_cols = circulation.shape[2]
    margin = 2 * SW_STEPS + 1
    both = jnp.concatenate([circulation, source_points.astype(jnp.float32)], axis=0)
    both = lax.all_gather(both, "band", axis=1, tiled=True)
    left, right = neighbours(both, "comp", 2, margin)
    wide = jnp.concatenate([left, both, right], axis=2)
    wide_cols = wide.shape[2]
    padded_cols = pl.cdiv(wide_cols, LANES) * LANES
    index = jnp.pad(wide[3:].astype(jnp.int32), ((0, 0), (0, 0), (0, padded_cols - wide_cols)))
    index = index.reshape(3, bands, tile_rows * padded_cols).transpose(1, 0, 2)

    increment, stress = exchange_sources(sent, quad_matrix, dissipation, coef, groups)
    own_stress = stress[:, :3].transpose(1, 0, 2).reshape(3, -1).astype(jnp.bfloat16)
    table = lax.all_gather(own_stress, ("band", "comp"), axis=0)
    table = table.reshape(bands, groups, 3, own_rows * columns // LANES, LANES)
    table = table.transpose(0, 2, 1, 3, 4).reshape(bands, 3, -1, LANES)
    cell_stress = pick(table, index).reshape(bands, 3, tile_rows, padded_cols)
    cell_stress = cell_stress.transpose(1, 0, 2, 3).reshape(3, -1, padded_cols)[..., :wide_cols]
    new_spectrum = finish(density, increment)

    global_col = (
        lax.axis_index("comp") * tile_cols - margin + jnp.arange(wide_cols, dtype=jnp.int32)
    )
    inside = ((global_col >= 0) & (global_col < tile_cols * groups)).astype(jnp.float32)[None, :]
    rimmed = jnp.pad(cell_stress * inside, ((0, 0), (1, 1), (1, 1)))
    force_down = -(diff_rows(rimmed[0]) + diff_cols(rimmed[1]))
    force_across = -(diff_rows(rimmed[1]) + diff_cols(rimmed[2]))
    height, flow_down, flow_across = wide[0], wide[1], wide[2]
    for repeat in range(SW_STEPS):
        down_ext = jnp.pad(flow_down, 1)
        across_ext = jnp.pad(flow_across, 1)
        height = (height - wave_speed * (diff_rows(down_ext) + diff_cols(across_ext))) * inside
        height_ext = jnp.pad(height, 1)
        flow_down = (
            (1.0 - friction) * flow_down
            - wave_speed * diff_rows(height_ext)
            + forcing_gain * force_down
        ) * inside
        flow_across = (
            (1.0 - friction) * flow_across
            - wave_speed * diff_cols(height_ext)
            + forcing_gain * force_across
        ) * inside
    stacked = jnp.stack([height, flow_down, flow_across])
    row_start = lax.axis_index("band") * tile_rows
    own = lax.dynamic_slice_in_dim(stacked, row_start, tile_rows, 1)
    return (new_spectrum, own[:, :, margin : margin + tile_cols])


def solution(mesh):
    in_specs = (
        P("comp", "band", None),
        P("band", None),
        P(),
        P(),
        P(None, "band", "comp"),
        P(None, "band", "comp"),
    )
    out_specs = (P("comp", "band", None), P(None, "band", "comp"))
    return jax.shard_map(
        on_device, mesh=mesh, in_specs=in_specs, out_specs=out_specs, check_vma=False
    )
```

```python
import functools
import math

import jax
import jax.numpy as jnp
from jax import lax
from jax.experimental import pallas as pl
from jax.experimental.pallas import tpu as pltpu
from jax.sharding import PartitionSpec as P

NF = 36
ND = 32
SUBSTEPS = 4
SRC_STEPS = 4
SW_STEPS = 8
COMP_BLOCK = 16
LANES = 128
VMEM_LIMIT = 50 * 1024 * 1024

step_source = 0.1
wave_speed = 0.35
friction = 0.05
forcing_gain = 0.15


def neighbours(cells, axis, dim, width):
    count = lax.axis_size(axis)
    ends = count - 1
    head = lax.slice_in_dim(cells, 0, width, axis=dim)
    tail = lax.slice_in_dim(cells, cells.shape[dim] - width, cells.shape[dim], axis=dim)
    before = lax.ppermute(tail, axis, [(i, i + 1) for i in range(ends)])
    after = lax.ppermute(head, axis, [(i + 1, i) for i in range(ends)])
    return before, after


def component_tables(offset, local_count, freqs, headings):
    indices = offset + jnp.arange(local_count, dtype=jnp.int32)
    frequency = (indices // headings).astype(jnp.float32)
    heading = (indices % headings).astype(jnp.float32)
    heading_angle = 2.0 * math.pi * (heading + 0.5) / headings
    fraction = (frequency + 0.5) / freqs
    group_speed = 0.25 + 0.4 * fraction
    wave_ratio = 0.5 + 0.5 * fraction
    cosine = jnp.cos(heading_angle)
    sine_part = jnp.sin(heading_angle)
    stress_coef = jnp.stack(
        [
            wave_ratio * (1.0 + cosine * cosine) - 0.5,
            wave_ratio * sine_part * cosine,
            wave_ratio * (1.0 + sine_part * sine_part) - 0.5,
        ]
    )
    return (group_speed * cosine, group_speed * sine_part, stress_coef)


def propagate_kernel(rows, *refs):
    x_refs = refs[:-6]
    before_ref, after_ref, wet_ref, speed_ref, dens_ref, sent_ref = refs[-6:]
    columns = dens_ref.shape[2]
    lane = lax.broadcasted_iota(jnp.int32, (8, columns), 1)
    before = before_ref[...].astype(jnp.float32)
    after = after_ref[...].astype(jnp.float32)
    total = rows + 2 * SUBSTEPS
    for half in range(COMP_BLOCK // 8):
        c0 = half * 8
        ax = jnp.broadcast_to(speed_ref[c0 : c0 + 8, 0:1], (8, columns))
        ay = jnp.broadcast_to(speed_ref[c0 : c0 + 8, 1:2], (8, columns))
        keep = 1.0 - jnp.abs(ax) - jnp.abs(ay)
        west, east = jnp.maximum(ax, 0.0), jnp.maximum(-ax, 0.0)
        south = jnp.where(lane > 0, jnp.maximum(ay, 0.0), 0.0)
        north = jnp.where(lane < columns - 1, jnp.maximum(-ay, 0.0), 0.0)
        stages = [dict() for _ in range(SUBSTEPS + 1)]
        for r in range(total):
            if r < SUBSTEPS:
                stages[0][r] = before[r, c0 : c0 + 8]
            elif r < SUBSTEPS + rows:
                part = pl.ds(c0 * rows + r - SUBSTEPS, 8, stride=rows)
                stages[0][r] = jnp.concatenate([x_ref[part, :] for x_ref in x_refs], axis=1)
            else:
                stages[0][r] = after[r - SUBSTEPS - rows, c0 : c0 + 8]
            for s in range(1, SUBSTEPS + 1):
                q = r - s
                if q < s or q >= total - s:
                    continue
                old = stages[s - 1]
                middle = old[q]
                value = (
                    keep * middle
                    + west * old[q - 1]
                    + east * old[q + 1]
                    + south * pltpu.roll(middle, 1, 1)
                    + north * pltpu.roll(middle, columns - 1, 1)
                ) * wet_ref[q : q + 1, :]
                stages[s][q] = value
                if s == SUBSTEPS:
                    dens_ref[q - SUBSTEPS, c0 : c0 + 8, :] = value
    sent_ref[...] = dens_ref[...].astype(jnp.bfloat16)


def propagate(spectrum, before, after, wet, speeds):
    count, rows, columns = spectrum.shape
    grid = (pl.cdiv(count, COMP_BLOCK),)
    parts = columns // LANES
    flat = spectrum.reshape(count * rows, columns)
    return pl.pallas_call(
        functools.partial(propagate_kernel, rows),
        grid=grid,
        in_specs=[
            pl.BlockSpec((COMP_BLOCK * rows, LANES), functools.partial(lambda p, i: (i, p), p))
            for p in range(parts)
        ]
        + [
            pl.BlockSpec((SUBSTEPS, COMP_BLOCK, columns), lambda i: (0, i, 0)),
            pl.BlockSpec((SUBSTEPS, COMP_BLOCK, columns), lambda i: (0, i, 0)),
            pl.BlockSpec((rows + 2 * SUBSTEPS, columns), lambda i: (0, 0)),
            pl.BlockSpec((COMP_BLOCK, 2), lambda i: (i, 0)),
        ],
        out_specs=[
            pl.BlockSpec((rows, COMP_BLOCK, columns), lambda i: (0, i, 0)),
            pl.BlockSpec((rows, COMP_BLOCK, columns), lambda i: (0, i, 0)),
        ],
        out_shape=[
            jax.ShapeDtypeStruct((rows, count, columns), jnp.float32),
            jax.ShapeDtypeStruct((rows, count, columns), jnp.bfloat16),
        ],
        compiler_params=pltpu.CompilerParams(vmem_limit_bytes=VMEM_LIMIT),
    )(*[flat] * parts, before, after, wet, speeds)


def finish_kernel(rows, dens_ref, inc_ref, out_ref, *parts):
    for r in range(rows):
        value = dens_ref[r] + inc_ref[r].astype(jnp.float32)
        for c0 in range(0, COMP_BLOCK, 8):
            for p, part in enumerate(parts):
                part[pl.ds(c0 * rows + r, 8, stride=rows), :] = value[
                    c0 : c0 + 8, p * LANES : (p + 1) * LANES
                ]
    for p, part in enumerate(parts):
        out_ref[:, p * LANES : (p + 1) * LANES] = part[...]


def finish(density, increment):
    rows, count, columns = density.shape
    spec = pl.BlockSpec((rows, COMP_BLOCK, columns), lambda i: (0, i, 0))
    out = pl.pallas_call(
        functools.partial(finish_kernel, rows),
        grid=(pl.cdiv(count, COMP_BLOCK),),
        in_specs=[spec, spec],
        out_specs=pl.BlockSpec((COMP_BLOCK * rows, columns), lambda i: (i, 0)),
        out_shape=jax.ShapeDtypeStruct((count * rows, columns), jnp.float32),
        scratch_shapes=[pltpu.VMEM((COMP_BLOCK * rows, LANES), jnp.float32)] * (columns // LANES),
        compiler_params=pltpu.CompilerParams(vmem_limit_bytes=VMEM_LIMIT),
    )(density, increment)
    return out.reshape(count, rows, columns)


def row_sources(base_ref, quad_ref, diss_ref, coef_ref, cur, low, inc_ref):
    blocks, count, columns = base_ref.shape
    total = blocks * count
    tiles = 3
    tile = total // tiles
    base = base_ref[...].reshape(total, columns)
    low[0] = base
    cur[...] = base.astype(jnp.float32)
    level = jnp.sum(cur[...], axis=0, keepdims=True)
    for s in range(SRC_STEPS):
        after = jnp.zeros_like(level)
        for t in range(tiles):
            part = slice(t * tile, (t + 1) * tile)
            product = jnp.dot(quad_ref[part, :], low[s % 2], preferred_element_type=jnp.float32)
            now = cur[part, :]
            now = now + step_source * now * (product - diss_ref[part, :] * (level / total))
            cur[part, :] = now
            after = after + jnp.sum(now, axis=0, keepdims=True)
            if s < SRC_STEPS - 1:
                low[(s + 1) % 2, part, :] = now.astype(jnp.bfloat16)
        level = after
    wide = base_ref[...].reshape(total, columns).astype(jnp.float32)
    increment = (cur[...] - wide).astype(jnp.bfloat16)
    inc_ref[...] = increment.reshape(blocks, count, columns)
    coupled = wide + increment.astype(jnp.float32)
    return (
        jnp.dot(
            coef_ref[...],
            coupled,
            precision=lax.Precision.HIGHEST,
            preferred_element_type=jnp.float32,
        )
        / total
    )


def sources_kernel(base_ref, quad_ref, diss_ref, coef_ref, inc_ref, stress_ref, cur, low):
    stress_ref[0] = row_sources(
        base_ref.at[:, 0], quad_ref, diss_ref, coef_ref, cur, low, inc_ref.at[:, 0]
    )


def sources(base, quad_matrix, dissipation, coef):
    blocks, rows, count, columns = base.shape
    total = blocks * count
    return pl.pallas_call(
        sources_kernel,
        grid=(rows,),
        in_specs=[
            pl.BlockSpec((blocks, 1, count, columns), lambda i: (0, i, 0, 0)),
            pl.BlockSpec((total, total), lambda i: (0, 0)),
            pl.BlockSpec((total, 1), lambda i: (0, 0)),
            pl.BlockSpec(coef.shape, lambda i: (0, 0)),
        ],
        out_specs=[
            pl.BlockSpec((blocks, 1, count, columns), lambda i: (0, i, 0, 0)),
            pl.BlockSpec((1, coef.shape[0], columns), lambda i: (i, 0, 0)),
        ],
        out_shape=[
            jax.ShapeDtypeStruct(base.shape, jnp.bfloat16),
            jax.ShapeDtypeStruct((rows, coef.shape[0], columns), jnp.float32),
        ],
        scratch_shapes=[
            pltpu.VMEM((total, columns), jnp.float32),
            pltpu.VMEM((2, total, columns), jnp.bfloat16),
        ],
        compiler_params=pltpu.CompilerParams(vmem_limit_bytes=VMEM_LIMIT),
    )(base, quad_matrix, dissipation, coef)


def pick_kernel(table_ref, index_ref, out_ref):
    high = table_ref.shape[2]
    cells = index_ref.shape[2]
    table = table_ref[0].reshape(3 * high, LANES)
    result = [jnp.zeros((1, cells), jnp.float32) for _ in range(3)]
    for m, weight in enumerate((0.5, 0.3, 0.2)):
        index = index_ref[0, m : m + 1, :]
        low = index % LANES
        top = index // LANES
        lane_hit = lax.broadcasted_iota(jnp.int32, (LANES, cells), 0) == low
        ones = jnp.where(lane_hit, 1.0, 0.0).astype(jnp.bfloat16)
        spread = jnp.dot(table, ones, preferred_element_type=jnp.float32)
        row_hit = lax.broadcasted_iota(jnp.int32, (high, cells), 0) == top
        for k in range(3):
            part = jnp.where(row_hit, spread[k * high : (k + 1) * high], 0.0)
            result[k] = result[k] + weight * jnp.sum(part, axis=0, keepdims=True)
    out_ref[0] = jnp.concatenate(result, axis=0)


def pick(table, index):
    bands, _, high, _ = table.shape
    cells = index.shape[2]
    return pl.pallas_call(
        pick_kernel,
        grid=(bands,),
        in_specs=[
            pl.BlockSpec((1, 3, high, LANES), lambda b: (b, 0, 0, 0)),
            pl.BlockSpec((1, 3, cells), lambda b: (b, 0, 0)),
        ],
        out_specs=pl.BlockSpec((1, 3, cells), lambda b: (b, 0, 0)),
        out_shape=jax.ShapeDtypeStruct((bands, 3, cells), jnp.float32),
        compiler_params=pltpu.CompilerParams(vmem_limit_bytes=VMEM_LIMIT),
    )(table, index)


def diff_rows(extended):
    return 0.5 * (extended[2:, 1:-1] - extended[:-2, 1:-1])


def diff_cols(extended):
    return 0.5 * (extended[1:-1, 2:] - extended[1:-1, :-2])


def coupled_kernel(sent, quad_ref, diss_ref, coef_ref, returned, table_ref, *scratch):
    land, incs, cur, low, lines, gath = scratch[:6]
    local_sem, push_send, push_recv, back_local, back_send, back_recv = scratch[6:12]
    band_send, band_recv, comp_send, comp_recv = scratch[12:]
    groups, own, count, columns = land.shape
    total = groups * count
    bands = gath.shape[1]
    me = lax.axis_index("comp")
    band = lax.axis_index("band")

    def comp_copy(src, dst, send, recv, peer):
        return pltpu.make_async_remote_copy(
            src_ref=src,
            dst_ref=dst,
            send_sem=send,
            recv_sem=recv,
            device_id=(peer, band),
            device_id_type=pl.DeviceIdType.MESH,
        )

    def band_copy(i, slot):
        return pltpu.make_async_remote_copy(
            src_ref=gath.at[me, band],
            dst_ref=gath.at[me, slot],
            send_sem=band_send.at[i],
            recv_sem=band_recv.at[i],
            device_id=(me, lax.rem(band + i, bands)),
            device_id_type=pl.DeviceIdType.MESH,
        )

    def to_peer(i):
        return lax.rem(me + i, groups)

    def from_peer(i):
        return lax.rem(me + groups - i, groups)

    def push(j, i, slot):
        peer = to_peer(i)
        return comp_copy(
            sent.at[peer * own + j], land.at[slot, j], push_send.at[j, i], push_recv.at[j, i], peer
        )

    def back(j, i, slot):
        peer = to_peer(i)
        return comp_copy(
            incs.at[peer, j],
            returned.at[slot * own + j],
            back_send.at[j, i],
            back_recv.at[j, i],
            peer,
        )

    def spread(i, slot):
        return comp_copy(gath.at[me], gath.at[slot], comp_send.at[i], comp_recv.at[i], to_peer(i))

    def push_local(j):
        return pltpu.make_async_copy(sent.at[me * own + j], land.at[me, j], local_sem.at[j])

    def back_own(j):
        return pltpu.make_async_copy(incs.at[me, j], returned.at[me * own + j], back_local.at[j])

    barrier = pltpu.get_barrier_semaphore()

    @pl.loop(1, groups)
    def _(i):
        pl.semaphore_signal(
            barrier, inc=1, device_id=(to_peer(i), band), device_id_type=pl.DeviceIdType.MESH
        )

    @pl.loop(1, bands)
    def _(i):
        pl.semaphore_signal(
            barrier,
            inc=1,
            device_id=(me, lax.rem(band + i, bands)),
            device_id_type=pl.DeviceIdType.MESH,
        )

    pl.semaphore_wait(barrier, groups + bands - 2)

    @pl.loop(0, own)
    def _(j):
        push_local(j).start()

        @pl.loop(1, groups)
        def _(i):
            push(j, i, me).start()

    tiles = 3
    tile = total // tiles

    @pl.loop(0, own)
    def _(j):
        push_local(j).wait()

        @pl.loop(1, groups)
        def _(i):
            push(j, i, from_peer(i)).wait_recv()

        base = land[:, j].reshape(total, columns)
        low[0] = base
        wide = base.astype(jnp.float32)
        cur[...] = wide

        def step(s, level):
            after = jnp.zeros_like(level)
            for t in range(tiles):
                part = slice(t * tile, (t + 1) * tile)
                product = jnp.dot(
                    quad_ref[part, :], low[lax.rem(s, 2)], preferred_element_type=jnp.float32
                )
                now = cur[part, :]
                now = now + step_source * now * (product - diss_ref[part, :] * (level / total))
                cur[part, :] = now
                after = after + jnp.sum(now, axis=0, keepdims=True)
                low[lax.rem(s + 1, 2), part, :] = now.astype(jnp.bfloat16)
            return after

        lax.fori_loop(0, SRC_STEPS, step, jnp.sum(wide, axis=0, keepdims=True))
        wide = land[:, j].reshape(total, columns).astype(jnp.float32)
        increment = (cur[...] - wide).astype(jnp.bfloat16)
        incs[:, j] = increment.reshape(groups, count, columns)
        back_own(j).start()

        @pl.loop(1, groups)
        def _(i):
            back(j, i, me).start()

        lines[j] = (
            jnp.dot(
                coef_ref[...],
                wide + increment.astype(jnp.float32),
                precision=lax.Precision.HIGHEST,
                preferred_element_type=jnp.float32,
            )
            / total
        )

    filled = [lines[j, 0:3] for j in range(own)]
    filled.append(jnp.zeros((gath.shape[2] - 3 * own, columns), jnp.float32))
    gath[me, band] = jnp.concatenate(filled, axis=0).astype(jnp.bfloat16)

    @pl.loop(1, bands)
    def _(i):
        band_copy(i, band).start()

    @pl.loop(1, bands)
    def _(i):
        band_copy(i, lax.rem(band + bands - i, bands)).wait_recv()

    @pl.loop(1, groups)
    def _(i):
        spread(i, me).start()

    @pl.loop(1, groups)
    def _(i):
        spread(i, from_peer(i)).wait_recv()

    table_ref[...] = gath[...]

    @pl.loop(1, bands)
    def _(i):
        band_copy(i, band).wait_send()

    @pl.loop(1, groups)
    def _(i):
        spread(i, me).wait_send()

    @pl.loop(0, own)
    def _(j):
        back_own(j).wait()

        @pl.loop(1, groups)
        def _(i):
            push(j, i, me).wait_send()
            back(j, i, me).wait_send()
            back(j, i, from_peer(i)).wait_recv()


def coupled(sent, quad_matrix, dissipation, coef, groups, bands):
    rows, count, columns = sent.shape
    own = rows // groups
    total = groups * count
    held = pl.cdiv(3 * own, 16) * 16
    vmem = pl.BlockSpec(memory_space=pltpu.VMEM)
    anywhere = pl.BlockSpec(memory_space=pl.ANY)
    pair = pltpu.SemaphoreType.DMA((own, groups))
    single = pltpu.SemaphoreType.DMA((own,))
    return pl.pallas_call(
        coupled_kernel,
        in_specs=[anywhere, vmem, vmem, vmem],
        out_specs=[anywhere, vmem],
        out_shape=[
            jax.ShapeDtypeStruct(sent.shape, jnp.bfloat16),
            jax.ShapeDtypeStruct((groups, bands, held, columns), jnp.bfloat16),
        ],
        scratch_shapes=[
            pltpu.VMEM((groups, own, count, columns), jnp.bfloat16),
            pltpu.VMEM((groups, own, count, columns), jnp.bfloat16),
            pltpu.VMEM((total, columns), jnp.float32),
            pltpu.VMEM((2, total, columns), jnp.bfloat16),
            pltpu.VMEM((own, coef.shape[0], columns), jnp.float32),
            pltpu.VMEM((groups, bands, held, columns), jnp.bfloat16),
            single,
            pair,
            pair,
            single,
            pair,
            pair,
            pltpu.SemaphoreType.DMA((bands,)),
            pltpu.SemaphoreType.DMA((bands,)),
            pltpu.SemaphoreType.DMA((groups,)),
            pltpu.SemaphoreType.DMA((groups,)),
        ],
        compiler_params=pltpu.CompilerParams(
            collective_id=0, has_side_effects=True, vmem_limit_bytes=VMEM_LIMIT
        ),
    )(sent, quad_matrix, dissipation[:, None], coef)


def exchange_sources(sent, quad_matrix, dissipation, coef, groups):
    rows, count, columns = sent.shape
    own = rows // groups
    arrived = lax.all_to_all(sent, "comp", split_axis=0, concat_axis=0, tiled=True)
    base = arrived.reshape(groups, own, count, columns)
    if count % 16:
        base = base.transpose(1, 0, 2, 3).reshape(1, own, groups * count, columns)
    increment, stress = sources(base, quad_matrix, dissipation[:, None], coef)
    if count % 16:
        increment = increment.reshape(own, groups, count, columns).transpose(1, 0, 2, 3)
    returned = lax.all_to_all(
        increment.reshape(rows, count, columns), "comp", split_axis=0, concat_axis=0, tiled=True
    )
    return returned, stress


def on_device(spectrum, wet_mask, quad_matrix, dissipation, circulation, source_points):
    local_count, row_count, columns = spectrum.shape
    groups = lax.axis_size("comp")
    bands = lax.axis_size("band")
    own_rows = row_count // groups
    offset = lax.axis_index("comp") * local_count
    speed_x, speed_y, _ = component_tables(offset, local_count, NF, ND)
    stress_coef = component_tables(0, local_count * groups, NF, ND)[2]
    coef = jnp.pad(stress_coef, ((0, 5), (0, 0)))

    head = spectrum[:, :SUBSTEPS].transpose(1, 0, 2).astype(jnp.bfloat16)
    tail = spectrum[:, row_count - SUBSTEPS :].transpose(1, 0, 2).astype(jnp.bfloat16)
    before, after = neighbours(jnp.concatenate([head, tail], axis=0), "band", 0, SUBSTEPS)
    wet = wet_mask.astype(jnp.float32)
    wet_before, wet_after = neighbours(wet, "band", 0, SUBSTEPS)
    wet = jnp.concatenate([wet_before, wet, wet_after], axis=0)
    density, sent = propagate(
        spectrum, before, after, wet, jnp.stack([speed_x, speed_y], axis=1)
    )

    tile_rows = circulation.shape[1]
    tile_cols = circulation.shape[2]
    margin = 2 * SW_STEPS + 1
    both = jnp.concatenate([circulation, source_points.astype(jnp.float32)], axis=0)
    both = lax.all_gather(both, "band", axis=1, tiled=True)
    left, right = neighbours(both, "comp", 2, margin)
    wide = jnp.concatenate([left, both, right], axis=2)
    wide_cols = wide.shape[2]
    padded_cols = pl.cdiv(wide_cols, LANES) * LANES
    index = jnp.pad(wide[3:].astype(jnp.int32), ((0, 0), (0, 0), (0, padded_cols - wide_cols)))
    index = index.reshape(3, bands, tile_rows * padded_cols).transpose(1, 0, 2)

    if local_count % 16:
        increment, stress = exchange_sources(sent, quad_matrix, dissipation, coef, groups)
        own_stress = stress[:, :3].astype(jnp.bfloat16)
        table = lax.all_gather(own_stress, "comp", axis=0)
        table = lax.all_gather(table, "band", axis=1)
    else:
        increment, table = coupled(sent, quad_matrix, dissipation, coef, groups, bands)
        table = table[:, :, : 3 * own_rows]
    table = table.reshape(groups, bands, own_rows, 3, columns // LANES, LANES)
    table = table.transpose(1, 3, 0, 2, 4, 5).reshape(bands, 3, -1, LANES)
    cell_stress = pick(table, index).reshape(bands, 3, tile_rows, padded_cols)
    cell_stress = cell_stress.transpose(1, 0, 2, 3).reshape(3, -1, padded_cols)[..., :wide_cols]
    new_spectrum = finish(density, increment)

    global_col = (
        lax.axis_index("comp") * tile_cols - margin + jnp.arange(wide_cols, dtype=jnp.int32)
    )
    inside = ((global_col >= 0) & (global_col < tile_cols * groups)).astype(jnp.float32)[None, :]
    rimmed = jnp.pad(cell_stress * inside, ((0, 0), (1, 1), (1, 1)))
    force_down = -(diff_rows(rimmed[0]) + diff_cols(rimmed[1]))
    force_across = -(diff_rows(rimmed[1]) + diff_cols(rimmed[2]))
    height, flow_down, flow_across = wide[0], wide[1], wide[2]
    for repeat in range(SW_STEPS):
        down_ext = jnp.pad(flow_down, 1)
        across_ext = jnp.pad(flow_across, 1)
        height = (height - wave_speed * (diff_rows(down_ext) + diff_cols(across_ext))) * inside
        height_ext = jnp.pad(height, 1)
        flow_down = (
            (1.0 - friction) * flow_down
            - wave_speed * diff_rows(height_ext)
            + forcing_gain * force_down
        ) * inside
        flow_across = (
            (1.0 - friction) * flow_across
            - wave_speed * diff_cols(height_ext)
            + forcing_gain * force_across
        ) * inside
    stacked = jnp.stack([height, flow_down, flow_across])
    row_start = lax.axis_index("band") * tile_rows
    own = lax.dynamic_slice_in_dim(stacked, row_start, tile_rows, 1)
    return (new_spectrum, own[:, :, margin : margin + tile_cols])


def solution(mesh):
    in_specs = (
        P("comp", "band", None),
        P("band", None),
        P(),
        P(),
        P(None, "band", "comp"),
        P(None, "band", "comp"),
    )
    out_specs = (P("comp", "band", None), P(None, "band", "comp"))
    return jax.shard_map(
        on_device, mesh=mesh, in_specs=in_specs, out_specs=out_specs, check_vma=False
    )
```

```python
import functools
import math

import jax
import jax.numpy as jnp
from jax import lax
from jax.experimental import pallas as pl
from jax.experimental.pallas import tpu as pltpu
from jax.sharding import PartitionSpec as P

NF = 36
ND = 32
SUBSTEPS = 4
SRC_STEPS = 4
SW_STEPS = 8
COMP_BLOCK = 16
LANES = 128
VMEM_LIMIT = 50 * 1024 * 1024

step_source = 0.1
wave_speed = 0.35
friction = 0.05
forcing_gain = 0.15


def neighbours(cells, axis, dim, width):
    count = lax.axis_size(axis)
    ends = count - 1
    head = lax.slice_in_dim(cells, 0, width, axis=dim)
    tail = lax.slice_in_dim(cells, cells.shape[dim] - width, cells.shape[dim], axis=dim)
    before = lax.ppermute(tail, axis, [(i, i + 1) for i in range(ends)])
    after = lax.ppermute(head, axis, [(i + 1, i) for i in range(ends)])
    return before, after


def component_tables(offset, local_count, freqs, headings):
    indices = offset + jnp.arange(local_count, dtype=jnp.int32)
    frequency = (indices // headings).astype(jnp.float32)
    heading = (indices % headings).astype(jnp.float32)
    heading_angle = 2.0 * math.pi * (heading + 0.5) / headings
    fraction = (frequency + 0.5) / freqs
    group_speed = 0.25 + 0.4 * fraction
    wave_ratio = 0.5 + 0.5 * fraction
    cosine = jnp.cos(heading_angle)
    sine_part = jnp.sin(heading_angle)
    stress_coef = jnp.stack(
        [
            wave_ratio * (1.0 + cosine * cosine) - 0.5,
            wave_ratio * sine_part * cosine,
            wave_ratio * (1.0 + sine_part * sine_part) - 0.5,
        ]
    )
    return (group_speed * cosine, group_speed * sine_part, stress_coef)


def propagate_kernel(rows, *refs):
    x_refs = refs[:-6]
    before_ref, after_ref, wet_ref, speed_ref, dens_ref, sent_ref = refs[-6:]
    columns = dens_ref.shape[2]
    lane = lax.broadcasted_iota(jnp.int32, (8, columns), 1)
    before = before_ref[...].astype(jnp.float32)
    after = after_ref[...].astype(jnp.float32)
    total = rows + 2 * SUBSTEPS
    for half in range(COMP_BLOCK // 8):
        c0 = half * 8
        ax = jnp.broadcast_to(speed_ref[c0 : c0 + 8, 0:1], (8, columns))
        ay = jnp.broadcast_to(speed_ref[c0 : c0 + 8, 1:2], (8, columns))
        keep = 1.0 - jnp.abs(ax) - jnp.abs(ay)
        west, east = jnp.maximum(ax, 0.0), jnp.maximum(-ax, 0.0)
        south = jnp.where(lane > 0, jnp.maximum(ay, 0.0), 0.0)
        north = jnp.where(lane < columns - 1, jnp.maximum(-ay, 0.0), 0.0)
        stages = [dict() for _ in range(SUBSTEPS + 1)]
        for r in range(total):
            if r < SUBSTEPS:
                stages[0][r] = before[r, c0 : c0 + 8]
            elif r < SUBSTEPS + rows:
                part = pl.ds(c0 * rows + r - SUBSTEPS, 8, stride=rows)
                stages[0][r] = jnp.concatenate([x_ref[part, :] for x_ref in x_refs], axis=1)
            else:
                stages[0][r] = after[r - SUBSTEPS - rows, c0 : c0 + 8]
            for s in range(1, SUBSTEPS + 1):
                q = r - s
                if q < s or q >= total - s:
                    continue
                old = stages[s - 1]
                middle = old[q]
                value = (
                    keep * middle
                    + west * old[q - 1]
                    + east * old[q + 1]
                    + south * pltpu.roll(middle, 1, 1)
                    + north * pltpu.roll(middle, columns - 1, 1)
                ) * wet_ref[q : q + 1, :]
                stages[s][q] = value
                if s == SUBSTEPS:
                    dens_ref[q - SUBSTEPS, c0 : c0 + 8, :] = value
    sent_ref[...] = dens_ref[...].astype(jnp.bfloat16)


def propagate(spectrum, before, after, wet, speeds):
    count, rows, columns = spectrum.shape
    grid = (pl.cdiv(count, COMP_BLOCK),)
    parts = columns // LANES
    flat = spectrum.reshape(count * rows, columns)
    return pl.pallas_call(
        functools.partial(propagate_kernel, rows),
        grid=grid,
        in_specs=[
            pl.BlockSpec((COMP_BLOCK * rows, LANES), functools.partial(lambda p, i: (i, p), p))
            for p in range(parts)
        ]
        + [
            pl.BlockSpec((SUBSTEPS, COMP_BLOCK, columns), lambda i: (0, i, 0)),
            pl.BlockSpec((SUBSTEPS, COMP_BLOCK, columns), lambda i: (0, i, 0)),
            pl.BlockSpec((rows + 2 * SUBSTEPS, columns), lambda i: (0, 0)),
            pl.BlockSpec((COMP_BLOCK, 2), lambda i: (i, 0)),
        ],
        out_specs=[
            pl.BlockSpec((rows, COMP_BLOCK, columns), lambda i: (0, i, 0)),
            pl.BlockSpec((rows, COMP_BLOCK, columns), lambda i: (0, i, 0)),
        ],
        out_shape=[
            jax.ShapeDtypeStruct((rows, count, columns), jnp.float32),
            jax.ShapeDtypeStruct((rows, count, columns), jnp.bfloat16),
        ],
        compiler_params=pltpu.CompilerParams(vmem_limit_bytes=VMEM_LIMIT),
    )(*[flat] * parts, before, after, wet, speeds)


def finish_kernel(rows, dens_ref, inc_ref, out_ref, *parts):
    for r in range(rows):
        value = dens_ref[r] + inc_ref[r].astype(jnp.float32)
        for c0 in range(0, COMP_BLOCK, 8):
            for p, part in enumerate(parts):
                part[pl.ds(c0 * rows + r, 8, stride=rows), :] = value[
                    c0 : c0 + 8, p * LANES : (p + 1) * LANES
                ]
    for p, part in enumerate(parts):
        out_ref[:, p * LANES : (p + 1) * LANES] = part[...]


def finish(density, increment):
    rows, count, columns = density.shape
    spec = pl.BlockSpec((rows, COMP_BLOCK, columns), lambda i: (0, i, 0))
    out = pl.pallas_call(
        functools.partial(finish_kernel, rows),
        grid=(pl.cdiv(count, COMP_BLOCK),),
        in_specs=[spec, spec],
        out_specs=pl.BlockSpec((COMP_BLOCK * rows, columns), lambda i: (i, 0)),
        out_shape=jax.ShapeDtypeStruct((count * rows, columns), jnp.float32),
        scratch_shapes=[pltpu.VMEM((COMP_BLOCK * rows, LANES), jnp.float32)] * (columns // LANES),
        compiler_params=pltpu.CompilerParams(vmem_limit_bytes=VMEM_LIMIT),
    )(density, increment)
    return out.reshape(count, rows, columns)


def row_sources(base_ref, quad_ref, diss_ref, coef_ref, cur, low, inc_ref):
    blocks, count, columns = base_ref.shape
    total = blocks * count
    tiles = 3
    tile = total // tiles
    base = base_ref[...].reshape(total, columns)
    low[0] = base
    cur[...] = base.astype(jnp.float32)
    level = jnp.sum(cur[...], axis=0, keepdims=True)
    for s in range(SRC_STEPS):
        after = jnp.zeros_like(level)
        for t in range(tiles):
            part = slice(t * tile, (t + 1) * tile)
            product = jnp.dot(quad_ref[part, :], low[s % 2], preferred_element_type=jnp.float32)
            now = cur[part, :]
            now = now + step_source * now * (product - diss_ref[part, :] * (level / total))
            cur[part, :] = now
            after = after + jnp.sum(now, axis=0, keepdims=True)
            if s < SRC_STEPS - 1:
                low[(s + 1) % 2, part, :] = now.astype(jnp.bfloat16)
        level = after
    wide = base_ref[...].reshape(total, columns).astype(jnp.float32)
    increment = (cur[...] - wide).astype(jnp.bfloat16)
    inc_ref[...] = increment.reshape(blocks, count, columns)
    coupled = wide + increment.astype(jnp.float32)
    return (
        jnp.dot(
            coef_ref[...],
            coupled,
            precision=lax.Precision.HIGHEST,
            preferred_element_type=jnp.float32,
        )
        / total
    )


def sources_kernel(base_ref, quad_ref, diss_ref, coef_ref, inc_ref, stress_ref, cur, low):
    stress_ref[0] = row_sources(
        base_ref.at[:, 0], quad_ref, diss_ref, coef_ref, cur, low, inc_ref.at[:, 0]
    )


def sources(base, quad_matrix, dissipation, coef):
    blocks, rows, count, columns = base.shape
    total = blocks * count
    return pl.pallas_call(
        sources_kernel,
        grid=(rows,),
        in_specs=[
            pl.BlockSpec((blocks, 1, count, columns), lambda i: (0, i, 0, 0)),
            pl.BlockSpec((total, total), lambda i: (0, 0)),
            pl.BlockSpec((total, 1), lambda i: (0, 0)),
            pl.BlockSpec(coef.shape, lambda i: (0, 0)),
        ],
        out_specs=[
            pl.BlockSpec((blocks, 1, count, columns), lambda i: (0, i, 0, 0)),
            pl.BlockSpec((1, coef.shape[0], columns), lambda i: (i, 0, 0)),
        ],
        out_shape=[
            jax.ShapeDtypeStruct(base.shape, jnp.bfloat16),
            jax.ShapeDtypeStruct((rows, coef.shape[0], columns), jnp.float32),
        ],
        scratch_shapes=[
            pltpu.VMEM((total, columns), jnp.float32),
            pltpu.VMEM((2, total, columns), jnp.bfloat16),
        ],
        compiler_params=pltpu.CompilerParams(vmem_limit_bytes=VMEM_LIMIT),
    )(base, quad_matrix, dissipation, coef)


def pick_kernel(table_ref, index_ref, out_ref):
    high = table_ref.shape[2]
    cells = index_ref.shape[2]
    table = table_ref[0].reshape(3 * high, LANES)
    result = [jnp.zeros((1, cells), jnp.float32) for _ in range(3)]
    for m, weight in enumerate((0.5, 0.3, 0.2)):
        index = index_ref[0, m : m + 1, :]
        low = index % LANES
        top = index // LANES
        lane_hit = lax.broadcasted_iota(jnp.int32, (LANES, cells), 0) == low
        ones = jnp.where(lane_hit, 1.0, 0.0).astype(jnp.bfloat16)
        spread = jnp.dot(table, ones, preferred_element_type=jnp.float32)
        row_hit = lax.broadcasted_iota(jnp.int32, (high, cells), 0) == top
        for k in range(3):
            part = jnp.where(row_hit, spread[k * high : (k + 1) * high], 0.0)
            result[k] = result[k] + weight * jnp.sum(part, axis=0, keepdims=True)
    out_ref[0] = jnp.concatenate(result, axis=0)


def pick(table, index):
    bands, _, high, _ = table.shape
    cells = index.shape[2]
    return pl.pallas_call(
        pick_kernel,
        grid=(bands,),
        in_specs=[
            pl.BlockSpec((1, 3, high, LANES), lambda b: (b, 0, 0, 0)),
            pl.BlockSpec((1, 3, cells), lambda b: (b, 0, 0)),
        ],
        out_specs=pl.BlockSpec((1, 3, cells), lambda b: (b, 0, 0)),
        out_shape=jax.ShapeDtypeStruct((bands, 3, cells), jnp.float32),
        compiler_params=pltpu.CompilerParams(vmem_limit_bytes=VMEM_LIMIT),
    )(table, index)


def diff_rows(extended):
    return 0.5 * (extended[2:, 1:-1] - extended[:-2, 1:-1])


def diff_cols(extended):
    return 0.5 * (extended[1:-1, 2:] - extended[1:-1, :-2])


def coupled_kernel(
    sent, quad_ref, diss_ref, coef_ref, both_ref, returned, table_ref, state_ref, *scratch
):
    land, incs, cur, low, lines, gath, hold = scratch[:7]
    scratch = scratch[1:]
    local_sem, push_send, push_recv, back_local, back_send, back_recv = scratch[6:12]
    band_send, band_recv, comp_send, comp_recv = scratch[12:16]
    tile_send, tile_recv, side_send, side_recv = scratch[16:]
    groups, own, count, columns = land.shape
    total = groups * count
    bands = gath.shape[1]
    me = lax.axis_index("comp")
    band = lax.axis_index("band")

    def comp_copy(src, dst, send, recv, peer):
        return pltpu.make_async_remote_copy(
            src_ref=src,
            dst_ref=dst,
            send_sem=send,
            recv_sem=recv,
            device_id=(peer, band),
            device_id_type=pl.DeviceIdType.MESH,
        )

    def band_copy(i, slot):
        return pltpu.make_async_remote_copy(
            src_ref=gath.at[me, band],
            dst_ref=gath.at[me, slot],
            send_sem=band_send.at[i],
            recv_sem=band_recv.at[i],
            device_id=(me, lax.rem(band + i, bands)),
            device_id_type=pl.DeviceIdType.MESH,
        )

    def to_peer(i):
        return lax.rem(me + i, groups)

    def from_peer(i):
        return lax.rem(me + groups - i, groups)

    def push(j, i, slot):
        peer = to_peer(i)
        return comp_copy(
            sent.at[peer * own + j], land.at[slot, j], push_send.at[j, i], push_recv.at[j, i], peer
        )

    def back(j, i, slot):
        peer = to_peer(i)
        return comp_copy(
            incs.at[peer, j],
            returned.at[slot * own + j],
            back_send.at[j, i],
            back_recv.at[j, i],
            peer,
        )

    def spread(i, slot):
        return comp_copy(gath.at[me], gath.at[slot], comp_send.at[i], comp_recv.at[i], to_peer(i))

    def tile_copy(i, slot):
        return pltpu.make_async_remote_copy(
            src_ref=hold.at[1, band],
            dst_ref=hold.at[1, slot],
            send_sem=tile_send.at[i],
            recv_sem=tile_recv.at[i],
            device_id=(me, lax.rem(band + i, bands)),
            device_id_type=pl.DeviceIdType.MESH,
        )

    def side_copy(k):
        peer = to_peer(1) if k == 0 else from_peer(1)
        return comp_copy(
            hold.at[1], hold.at[2 * k], side_send.at[k], side_recv.at[k], peer
        )

    def push_local(j):
        return pltpu.make_async_copy(sent.at[me * own + j], land.at[me, j], local_sem.at[j])

    def back_own(j):
        return pltpu.make_async_copy(incs.at[me, j], returned.at[me * own + j], back_local.at[j])

    barrier = pltpu.get_barrier_semaphore()

    @pl.loop(1, groups)
    def _(i):
        pl.semaphore_signal(
            barrier, inc=1, device_id=(to_peer(i), band), device_id_type=pl.DeviceIdType.MESH
        )

    @pl.loop(1, bands)
    def _(i):
        pl.semaphore_signal(
            barrier,
            inc=1,
            device_id=(me, lax.rem(band + i, bands)),
            device_id_type=pl.DeviceIdType.MESH,
        )

    pl.semaphore_wait(barrier, groups + bands - 2)

    hold[1, band] = both_ref[...]

    @pl.loop(1, bands)
    def _(i):
        tile_copy(i, band).start()

    @pl.loop(0, own)
    def _(j):
        push_local(j).start()

        @pl.loop(1, groups)
        def _(i):
            push(j, i, me).start()

    @pl.loop(1, bands)
    def _(i):
        tile_copy(i, lax.rem(band + bands - i, bands)).wait_recv()

    side_copy(0).start()
    side_copy(1).start()

    tiles = 3
    tile = total // tiles

    @pl.loop(0, own)
    def _(j):
        push_local(j).wait()

        @pl.loop(1, groups)
        def _(i):
            push(j, i, from_peer(i)).wait_recv()

        base = land[:, j].reshape(total, columns)
        low[0] = base
        wide = base.astype(jnp.float32)
        cur[...] = wide

        def step(s, level):
            after = jnp.zeros_like(level)
            for t in range(tiles):
                part = slice(t * tile, (t + 1) * tile)
                product = jnp.dot(
                    quad_ref[part, :], low[lax.rem(s, 2)], preferred_element_type=jnp.float32
                )
                now = cur[part, :]
                now = now + step_source * now * (product - diss_ref[part, :] * (level / total))
                cur[part, :] = now
                after = after + jnp.sum(now, axis=0, keepdims=True)
                low[lax.rem(s + 1, 2), part, :] = now.astype(jnp.bfloat16)
            return after

        lax.fori_loop(0, SRC_STEPS, step, jnp.sum(wide, axis=0, keepdims=True))
        wide = land[:, j].reshape(total, columns).astype(jnp.float32)
        increment = (cur[...] - wide).astype(jnp.bfloat16)
        incs[:, j] = increment.reshape(groups, count, columns)
        back_own(j).start()

        @pl.loop(1, groups)
        def _(i):
            back(j, i, me).start()

        lines[j] = (
            jnp.dot(
                coef_ref[...],
                wide + increment.astype(jnp.float32),
                precision=lax.Precision.HIGHEST,
                preferred_element_type=jnp.float32,
            )
            / total
        )

    filled = [lines[j, 0:3] for j in range(own)]
    filled.append(jnp.zeros((gath.shape[2] - 3 * own, columns), jnp.float32))
    gath[me, band] = jnp.concatenate(filled, axis=0).astype(jnp.bfloat16)

    @pl.loop(1, bands)
    def _(i):
        band_copy(i, band).start()

    @pl.loop(1, bands)
    def _(i):
        band_copy(i, lax.rem(band + bands - i, bands)).wait_recv()

    @pl.loop(1, groups)
    def _(i):
        spread(i, me).start()

    @pl.loop(1, groups)
    def _(i):
        spread(i, from_peer(i)).wait_recv()

    table_ref[...] = gath[...]
    side_copy(0).wait()
    side_copy(1).wait()
    state_ref[...] = hold[...]

    @pl.loop(1, bands)
    def _(i):
        tile_copy(i, band).wait_send()
        band_copy(i, band).wait_send()

    @pl.loop(1, groups)
    def _(i):
        spread(i, me).wait_send()

    @pl.loop(0, own)
    def _(j):
        back_own(j).wait()

        @pl.loop(1, groups)
        def _(i):
            push(j, i, me).wait_send()
            back(j, i, me).wait_send()
            back(j, i, from_peer(i)).wait_recv()


def coupled(sent, quad_matrix, dissipation, coef, both, groups, bands):
    rows, count, columns = sent.shape
    own = rows // groups
    total = groups * count
    held = pl.cdiv(3 * own, 16) * 16
    vmem = pl.BlockSpec(memory_space=pltpu.VMEM)
    anywhere = pl.BlockSpec(memory_space=pl.ANY)
    pair = pltpu.SemaphoreType.DMA((own, groups))
    single = pltpu.SemaphoreType.DMA((own,))
    return pl.pallas_call(
        coupled_kernel,
        in_specs=[anywhere, vmem, vmem, vmem, vmem],
        out_specs=[anywhere, vmem, vmem],
        out_shape=[
            jax.ShapeDtypeStruct(sent.shape, jnp.bfloat16),
            jax.ShapeDtypeStruct((groups, bands, held, columns), jnp.bfloat16),
            jax.ShapeDtypeStruct((3, bands) + both.shape, jnp.float32),
        ],
        scratch_shapes=[
            pltpu.VMEM((groups, own, count, columns), jnp.bfloat16),
            pltpu.VMEM((groups, own, count, columns), jnp.bfloat16),
            pltpu.VMEM((total, columns), jnp.float32),
            pltpu.VMEM((2, total, columns), jnp.bfloat16),
            pltpu.VMEM((own, coef.shape[0], columns), jnp.float32),
            pltpu.VMEM((groups, bands, held, columns), jnp.bfloat16),
            pltpu.VMEM((3, bands) + both.shape, jnp.float32),
            single,
            pair,
            pair,
            single,
            pair,
            pair,
            pltpu.SemaphoreType.DMA((bands,)),
            pltpu.SemaphoreType.DMA((bands,)),
            pltpu.SemaphoreType.DMA((groups,)),
            pltpu.SemaphoreType.DMA((groups,)),
            pltpu.SemaphoreType.DMA((bands,)),
            pltpu.SemaphoreType.DMA((bands,)),
            pltpu.SemaphoreType.DMA((2,)),
            pltpu.SemaphoreType.DMA((2,)),
        ],
        compiler_params=pltpu.CompilerParams(
            collective_id=0, has_side_effects=True, vmem_limit_bytes=VMEM_LIMIT
        ),
    )(sent, quad_matrix, dissipation[:, None], coef, both)


def exchange_sources(sent, quad_matrix, dissipation, coef, groups):
    rows, count, columns = sent.shape
    own = rows // groups
    arrived = lax.all_to_all(sent, "comp", split_axis=0, concat_axis=0, tiled=True)
    base = arrived.reshape(groups, own, count, columns)
    if count % 16:
        base = base.transpose(1, 0, 2, 3).reshape(1, own, groups * count, columns)
    increment, stress = sources(base, quad_matrix, dissipation[:, None], coef)
    if count % 16:
        increment = increment.reshape(own, groups, count, columns).transpose(1, 0, 2, 3)
    returned = lax.all_to_all(
        increment.reshape(rows, count, columns), "comp", split_axis=0, concat_axis=0, tiled=True
    )
    return returned, stress


def on_device(spectrum, wet_mask, quad_matrix, dissipation, circulation, source_points):
    local_count, row_count, columns = spectrum.shape
    groups = lax.axis_size("comp")
    bands = lax.axis_size("band")
    own_rows = row_count // groups
    offset = lax.axis_index("comp") * local_count
    speed_x, speed_y, _ = component_tables(offset, local_count, NF, ND)
    stress_coef = component_tables(0, local_count * groups, NF, ND)[2]
    coef = jnp.pad(stress_coef, ((0, 5), (0, 0)))

    head = spectrum[:, :SUBSTEPS].transpose(1, 0, 2).astype(jnp.bfloat16)
    tail = spectrum[:, row_count - SUBSTEPS :].transpose(1, 0, 2).astype(jnp.bfloat16)
    ends = jnp.concatenate([head, tail], axis=0)
    wet = wet_mask.astype(jnp.float32)
    wet_ends = jnp.concatenate([wet[:SUBSTEPS], wet[row_count - SUBSTEPS :]], axis=0)
    ends = jnp.concatenate([ends, wet_ends.astype(jnp.bfloat16)[:, None]], axis=1)
    before, after = neighbours(ends, "band", 0, SUBSTEPS)
    wet_before = before[:, local_count].astype(jnp.float32)
    wet_after = after[:, local_count].astype(jnp.float32)
    wet = jnp.concatenate([wet_before, wet, wet_after], axis=0)
    density, sent = propagate(
        spectrum, before, after, wet, jnp.stack([speed_x, speed_y], axis=1)
    )

    tile_rows = circulation.shape[1]
    tile_cols = circulation.shape[2]
    margin = 2 * SW_STEPS + 1
    both = jnp.concatenate([circulation, source_points.astype(jnp.float32)], axis=0)
    if local_count % 16:
        increment, stress = exchange_sources(sent, quad_matrix, dissipation, coef, groups)
        own_stress = stress[:, :3].astype(jnp.bfloat16)
        table = lax.all_gather(own_stress, "comp", axis=0)
        table = lax.all_gather(table, "band", axis=1)
        both = lax.all_gather(both, "band", axis=1, tiled=True)
        left, right = neighbours(both, "comp", 2, margin)
    else:
        increment, table, state = coupled(
            sent, quad_matrix, dissipation, coef, both, groups, bands
        )
        table = table[:, :, : 3 * own_rows]
        state = state.transpose(0, 2, 1, 3, 4).reshape(3, 6, bands * tile_rows, tile_cols)
        left, both, right = state[0, ..., tile_cols - margin :], state[1], state[2, ..., :margin]
    wide = jnp.concatenate([left, both, right], axis=2)
    wide_cols = wide.shape[2]
    padded_cols = pl.cdiv(wide_cols, LANES) * LANES
    index = jnp.pad(wide[3:].astype(jnp.int32), ((0, 0), (0, 0), (0, padded_cols - wide_cols)))
    index = index.reshape(3, bands, tile_rows * padded_cols).transpose(1, 0, 2)
    table = table.reshape(groups, bands, own_rows, 3, columns // LANES, LANES)
    table = table.transpose(1, 3, 0, 2, 4, 5).reshape(bands, 3, -1, LANES)
    cell_stress = pick(table, index).reshape(bands, 3, tile_rows, padded_cols)
    cell_stress = cell_stress.transpose(1, 0, 2, 3).reshape(3, -1, padded_cols)[..., :wide_cols]
    new_spectrum = finish(density, increment)

    global_col = (
        lax.axis_index("comp") * tile_cols - margin + jnp.arange(wide_cols, dtype=jnp.int32)
    )
    inside = ((global_col >= 0) & (global_col < tile_cols * groups)).astype(jnp.float32)[None, :]
    rimmed = jnp.pad(cell_stress * inside, ((0, 0), (1, 1), (1, 1)))
    force_down = -(diff_rows(rimmed[0]) + diff_cols(rimmed[1]))
    force_across = -(diff_rows(rimmed[1]) + diff_cols(rimmed[2]))
    height, flow_down, flow_across = wide[0] * inside, wide[1] * inside, wide[2] * inside
    for repeat in range(SW_STEPS):
        down_ext = jnp.pad(flow_down, 1)
        across_ext = jnp.pad(flow_across, 1)
        height = (height - wave_speed * (diff_rows(down_ext) + diff_cols(across_ext))) * inside
        height_ext = jnp.pad(height, 1)
        flow_down = (
            (1.0 - friction) * flow_down
            - wave_speed * diff_rows(height_ext)
            + forcing_gain * force_down
        ) * inside
        flow_across = (
            (1.0 - friction) * flow_across
            - wave_speed * diff_cols(height_ext)
            + forcing_gain * force_across
        ) * inside
    stacked = jnp.stack([height, flow_down, flow_across])
    row_start = lax.axis_index("band") * tile_rows
    own = lax.dynamic_slice_in_dim(stacked, row_start, tile_rows, 1)
    return (new_spectrum, own[:, :, margin : margin + tile_cols])


def solution(mesh):
    in_specs = (
        P("comp", "band", None),
        P("band", None),
        P(),
        P(),
        P(None, "band", "comp"),
        P(None, "band", "comp"),
    )
    out_specs = (P("comp", "band", None), P(None, "band", "comp"))
    return jax.shard_map(
        on_device, mesh=mesh, in_specs=in_specs, out_specs=out_specs, check_vma=False
    )
```

```python
import functools
import math

import jax
import jax.numpy as jnp
from jax import lax
from jax.experimental import pallas as pl
from jax.experimental.pallas import tpu as pltpu
from jax.sharding import PartitionSpec as P

NF = 36
ND = 32
SUBSTEPS = 4
SRC_STEPS = 4
SW_STEPS = 8
COMP_BLOCK = 16
LANES = 128
VMEM_LIMIT = 50 * 1024 * 1024

step_source = 0.1
wave_speed = 0.35
friction = 0.05
forcing_gain = 0.15


def neighbours(cells, axis, dim, width):
    count = lax.axis_size(axis)
    ends = count - 1
    head = lax.slice_in_dim(cells, 0, width, axis=dim)
    tail = lax.slice_in_dim(cells, cells.shape[dim] - width, cells.shape[dim], axis=dim)
    before = lax.ppermute(tail, axis, [(i, i + 1) for i in range(ends)])
    after = lax.ppermute(head, axis, [(i + 1, i) for i in range(ends)])
    return before, after


def component_tables(offset, local_count, freqs, headings):
    indices = offset + jnp.arange(local_count, dtype=jnp.int32)
    frequency = (indices // headings).astype(jnp.float32)
    heading = (indices % headings).astype(jnp.float32)
    heading_angle = 2.0 * math.pi * (heading + 0.5) / headings
    fraction = (frequency + 0.5) / freqs
    group_speed = 0.25 + 0.4 * fraction
    wave_ratio = 0.5 + 0.5 * fraction
    cosine = jnp.cos(heading_angle)
    sine_part = jnp.sin(heading_angle)
    stress_coef = jnp.stack(
        [
            wave_ratio * (1.0 + cosine * cosine) - 0.5,
            wave_ratio * sine_part * cosine,
            wave_ratio * (1.0 + sine_part * sine_part) - 0.5,
        ]
    )
    return (group_speed * cosine, group_speed * sine_part, stress_coef)


def propagate_kernel(rows, *refs):
    x_refs = refs[:-6]
    before_ref, after_ref, wet_ref, speed_ref, dens_ref, sent_ref = refs[-6:]
    columns = dens_ref.shape[2]
    lane = lax.broadcasted_iota(jnp.int32, (8, columns), 1)
    before = before_ref[...].astype(jnp.float32)
    after = after_ref[...].astype(jnp.float32)
    total = rows + 2 * SUBSTEPS
    halves = []
    for c0 in range(0, COMP_BLOCK, 8):
        ax = jnp.broadcast_to(speed_ref[c0 : c0 + 8, 0:1], (8, columns))
        ay = jnp.broadcast_to(speed_ref[c0 : c0 + 8, 1:2], (8, columns))
        keep = 1.0 - jnp.abs(ax) - jnp.abs(ay)
        west, east = jnp.maximum(ax, 0.0), jnp.maximum(-ax, 0.0)
        south = jnp.where(lane > 0, jnp.maximum(ay, 0.0), 0.0)
        north = jnp.where(lane < columns - 1, jnp.maximum(-ay, 0.0), 0.0)
        stages = [dict() for _ in range(SUBSTEPS + 1)]
        halves.append((c0, keep, west, east, south, north, stages))
    for r in range(total + SUBSTEPS):
        for c0, keep, west, east, south, north, stages in halves:
            if r < SUBSTEPS:
                stages[0][r] = before[r, c0 : c0 + 8]
            elif r < SUBSTEPS + rows:
                part = pl.ds(c0 * rows + r - SUBSTEPS, 8, stride=rows)
                stages[0][r] = jnp.concatenate([x_ref[part, :] for x_ref in x_refs], axis=1)
            elif r < total:
                stages[0][r] = after[r - SUBSTEPS - rows, c0 : c0 + 8]
            for s in range(SUBSTEPS, 0, -1):
                q = r - 2 * s
                if q < s or q >= total - s:
                    continue
                old = stages[s - 1]
                middle = old[q]
                value = (
                    keep * middle
                    + west * old[q - 1]
                    + east * old[q + 1]
                    + south * pltpu.roll(middle, 1, 1)
                    + north * pltpu.roll(middle, columns - 1, 1)
                ) * wet_ref[q : q + 1, :]
                stages[s][q] = value
                if s == SUBSTEPS:
                    dens_ref[q - SUBSTEPS, c0 : c0 + 8, :] = value
    sent_ref[...] = dens_ref[...].astype(jnp.bfloat16)


def propagate(spectrum, before, after, wet, speeds):
    count, rows, columns = spectrum.shape
    grid = (pl.cdiv(count, COMP_BLOCK),)
    parts = columns // LANES
    flat = spectrum.reshape(count * rows, columns)
    return pl.pallas_call(
        functools.partial(propagate_kernel, rows),
        grid=grid,
        in_specs=[
            pl.BlockSpec((COMP_BLOCK * rows, LANES), functools.partial(lambda p, i: (i, p), p))
            for p in range(parts)
        ]
        + [
            pl.BlockSpec((SUBSTEPS, COMP_BLOCK, columns), lambda i: (0, i, 0)),
            pl.BlockSpec((SUBSTEPS, COMP_BLOCK, columns), lambda i: (0, i, 0)),
            pl.BlockSpec((rows + 2 * SUBSTEPS, columns), lambda i: (0, 0)),
            pl.BlockSpec((COMP_BLOCK, 2), lambda i: (i, 0)),
        ],
        out_specs=[
            pl.BlockSpec((rows, COMP_BLOCK, columns), lambda i: (0, i, 0)),
            pl.BlockSpec((rows, COMP_BLOCK, columns), lambda i: (0, i, 0)),
        ],
        out_shape=[
            jax.ShapeDtypeStruct((rows, count, columns), jnp.float32),
            jax.ShapeDtypeStruct((rows, count, columns), jnp.bfloat16),
        ],
        compiler_params=pltpu.CompilerParams(vmem_limit_bytes=VMEM_LIMIT),
    )(*[flat] * parts, before, after, wet, speeds)


def finish_kernel(rows, dens_ref, inc_ref, out_ref, *parts):
    for r in range(rows):
        value = dens_ref[r] + inc_ref[r].astype(jnp.float32)
        for c0 in range(0, COMP_BLOCK, 8):
            for p, part in enumerate(parts):
                part[pl.ds(c0 * rows + r, 8, stride=rows), :] = value[
                    c0 : c0 + 8, p * LANES : (p + 1) * LANES
                ]
    for p, part in enumerate(parts):
        out_ref[:, p * LANES : (p + 1) * LANES] = part[...]


def finish(density, increment):
    rows, count, columns = density.shape
    spec = pl.BlockSpec((rows, COMP_BLOCK, columns), lambda i: (0, i, 0))
    out = pl.pallas_call(
        functools.partial(finish_kernel, rows),
        grid=(pl.cdiv(count, COMP_BLOCK),),
        in_specs=[spec, spec],
        out_specs=pl.BlockSpec((COMP_BLOCK * rows, columns), lambda i: (i, 0)),
        out_shape=jax.ShapeDtypeStruct((count * rows, columns), jnp.float32),
        scratch_shapes=[pltpu.VMEM((COMP_BLOCK * rows, LANES), jnp.float32)] * (columns // LANES),
        compiler_params=pltpu.CompilerParams(vmem_limit_bytes=VMEM_LIMIT),
    )(density, increment)
    return out.reshape(count, rows, columns)


def row_sources(base_ref, quad_ref, diss_ref, coef_ref, cur, low, inc_ref):
    blocks, count, columns = base_ref.shape
    total = blocks * count
    tiles = 3
    tile = total // tiles
    base = base_ref[...].reshape(total, columns)
    low[0] = base
    cur[...] = base.astype(jnp.float32)
    level = jnp.sum(cur[...], axis=0, keepdims=True)
    for s in range(SRC_STEPS):
        after = jnp.zeros_like(level)
        for t in range(tiles):
            part = slice(t * tile, (t + 1) * tile)
            product = jnp.dot(quad_ref[part, :], low[s % 2], preferred_element_type=jnp.float32)
            now = cur[part, :]
            now = now + step_source * now * (product - diss_ref[part, :] * (level / total))
            cur[part, :] = now
            after = after + jnp.sum(now, axis=0, keepdims=True)
            if s < SRC_STEPS - 1:
                low[(s + 1) % 2, part, :] = now.astype(jnp.bfloat16)
        level = after
    wide = base_ref[...].reshape(total, columns).astype(jnp.float32)
    increment = (cur[...] - wide).astype(jnp.bfloat16)
    inc_ref[...] = increment.reshape(blocks, count, columns)
    coupled = wide + increment.astype(jnp.float32)
    return (
        jnp.dot(
            coef_ref[...],
            coupled,
            precision=lax.Precision.HIGHEST,
            preferred_element_type=jnp.float32,
        )
        / total
    )


def sources_kernel(base_ref, quad_ref, diss_ref, coef_ref, inc_ref, stress_ref, cur, low):
    stress_ref[0] = row_sources(
        base_ref.at[:, 0], quad_ref, diss_ref, coef_ref, cur, low, inc_ref.at[:, 0]
    )


def sources(base, quad_matrix, dissipation, coef):
    blocks, rows, count, columns = base.shape
    total = blocks * count
    return pl.pallas_call(
        sources_kernel,
        grid=(rows,),
        in_specs=[
            pl.BlockSpec((blocks, 1, count, columns), lambda i: (0, i, 0, 0)),
            pl.BlockSpec((total, total), lambda i: (0, 0)),
            pl.BlockSpec((total, 1), lambda i: (0, 0)),
            pl.BlockSpec(coef.shape, lambda i: (0, 0)),
        ],
        out_specs=[
            pl.BlockSpec((blocks, 1, count, columns), lambda i: (0, i, 0, 0)),
            pl.BlockSpec((1, coef.shape[0], columns), lambda i: (i, 0, 0)),
        ],
        out_shape=[
            jax.ShapeDtypeStruct(base.shape, jnp.bfloat16),
            jax.ShapeDtypeStruct((rows, coef.shape[0], columns), jnp.float32),
        ],
        scratch_shapes=[
            pltpu.VMEM((total, columns), jnp.float32),
            pltpu.VMEM((2, total, columns), jnp.bfloat16),
        ],
        compiler_params=pltpu.CompilerParams(vmem_limit_bytes=VMEM_LIMIT),
    )(base, quad_matrix, dissipation, coef)


def pick_kernel(table_ref, index_ref, out_ref):
    high = table_ref.shape[2]
    cells = index_ref.shape[2]
    table = table_ref[0].reshape(3 * high, LANES)
    result = [jnp.zeros((1, cells), jnp.float32) for _ in range(3)]
    for m, weight in enumerate((0.5, 0.3, 0.2)):
        index = index_ref[0, m : m + 1, :]
        low = index % LANES
        top = index // LANES
        lane_hit = lax.broadcasted_iota(jnp.int32, (LANES, cells), 0) == low
        ones = jnp.where(lane_hit, 1.0, 0.0).astype(jnp.bfloat16)
        spread = jnp.dot(table, ones, preferred_element_type=jnp.float32)
        row_hit = lax.broadcasted_iota(jnp.int32, (high, cells), 0) == top
        for k in range(3):
            part = jnp.where(row_hit, spread[k * high : (k + 1) * high], 0.0)
            result[k] = result[k] + weight * jnp.sum(part, axis=0, keepdims=True)
    out_ref[0] = jnp.concatenate(result, axis=0)


def pick(table, index):
    bands, _, high, _ = table.shape
    cells = index.shape[2]
    return pl.pallas_call(
        pick_kernel,
        grid=(bands,),
        in_specs=[
            pl.BlockSpec((1, 3, high, LANES), lambda b: (b, 0, 0, 0)),
            pl.BlockSpec((1, 3, cells), lambda b: (b, 0, 0)),
        ],
        out_specs=pl.BlockSpec((1, 3, cells), lambda b: (b, 0, 0)),
        out_shape=jax.ShapeDtypeStruct((bands, 3, cells), jnp.float32),
        compiler_params=pltpu.CompilerParams(vmem_limit_bytes=VMEM_LIMIT),
    )(table, index)


def diff_rows(extended):
    return 0.5 * (extended[2:, 1:-1] - extended[:-2, 1:-1])


def diff_cols(extended):
    return 0.5 * (extended[1:-1, 2:] - extended[1:-1, :-2])


def coupled_kernel(
    sent, quad_ref, diss_ref, coef_ref, both_ref, returned, table_ref, state_ref, *scratch
):
    land, incs, cur, low, lines, gath, hold = scratch[:7]
    scratch = scratch[1:]
    local_sem, push_send, push_recv, back_local, back_send, back_recv = scratch[6:12]
    band_send, band_recv, comp_send, comp_recv = scratch[12:16]
    tile_send, tile_recv, side_send, side_recv = scratch[16:]
    groups, own, count, columns = land.shape
    total = groups * count
    bands = gath.shape[1]
    me = lax.axis_index("comp")
    band = lax.axis_index("band")

    def comp_copy(src, dst, send, recv, peer):
        return pltpu.make_async_remote_copy(
            src_ref=src,
            dst_ref=dst,
            send_sem=send,
            recv_sem=recv,
            device_id=(peer, band),
            device_id_type=pl.DeviceIdType.MESH,
        )

    def band_copy(i, slot):
        return pltpu.make_async_remote_copy(
            src_ref=gath.at[me, band],
            dst_ref=gath.at[me, slot],
            send_sem=band_send.at[i],
            recv_sem=band_recv.at[i],
            device_id=(me, lax.rem(band + i, bands)),
            device_id_type=pl.DeviceIdType.MESH,
        )

    def to_peer(i):
        return lax.rem(me + i, groups)

    def from_peer(i):
        return lax.rem(me + groups - i, groups)

    def push(j, i, slot):
        peer = to_peer(i)
        return comp_copy(
            sent.at[peer * own + j], land.at[slot, j], push_send.at[j, i], push_recv.at[j, i], peer
        )

    def back(j, i, slot):
        peer = to_peer(i)
        return comp_copy(
            incs.at[peer, j],
            returned.at[slot * own + j],
            back_send.at[j, i],
            back_recv.at[j, i],
            peer,
        )

    def spread(i, slot):
        return comp_copy(gath.at[me], gath.at[slot], comp_send.at[i], comp_recv.at[i], to_peer(i))

    def tile_copy(i, slot):
        return pltpu.make_async_remote_copy(
            src_ref=hold.at[1, band],
            dst_ref=hold.at[1, slot],
            send_sem=tile_send.at[i],
            recv_sem=tile_recv.at[i],
            device_id=(me, lax.rem(band + i, bands)),
            device_id_type=pl.DeviceIdType.MESH,
        )

    def side_copy(k):
        peer = to_peer(1) if k == 0 else from_peer(1)
        return comp_copy(
            hold.at[1], hold.at[2 * k], side_send.at[k], side_recv.at[k], peer
        )

    def push_local(j):
        return pltpu.make_async_copy(sent.at[me * own + j], land.at[me, j], local_sem.at[j])

    def back_own(j):
        return pltpu.make_async_copy(incs.at[me, j], returned.at[me * own + j], back_local.at[j])

    barrier = pltpu.get_barrier_semaphore()

    @pl.loop(1, groups)
    def _(i):
        pl.semaphore_signal(
            barrier, inc=1, device_id=(to_peer(i), band), device_id_type=pl.DeviceIdType.MESH
        )

    @pl.loop(1, bands)
    def _(i):
        pl.semaphore_signal(
            barrier,
            inc=1,
            device_id=(me, lax.rem(band + i, bands)),
            device_id_type=pl.DeviceIdType.MESH,
        )

    pl.semaphore_wait(barrier, groups + bands - 2)

    hold[1, band] = both_ref[...]

    @pl.loop(1, bands)
    def _(i):
        tile_copy(i, band).start()

    @pl.loop(0, own)
    def _(j):
        push_local(j).start()

        @pl.loop(1, groups)
        def _(i):
            push(j, i, me).start()

    @pl.loop(1, bands)
    def _(i):
        tile_copy(i, lax.rem(band + bands - i, bands)).wait_recv()

    side_copy(0).start()
    side_copy(1).start()

    tiles = 3
    tile = total // tiles

    @pl.loop(0, own)
    def _(j):
        push_local(j).wait()

        @pl.loop(1, groups)
        def _(i):
            push(j, i, from_peer(i)).wait_recv()

        base = land[:, j].reshape(total, columns)
        low[0] = base
        wide = base.astype(jnp.float32)
        cur[...] = wide

        def step(s, level):
            after = jnp.zeros_like(level)
            for t in range(tiles):
                part = slice(t * tile, (t + 1) * tile)
                product = jnp.dot(
                    quad_ref[part, :], low[lax.rem(s, 2)], preferred_element_type=jnp.float32
                )
                now = cur[part, :]
                now = now + step_source * now * (product - diss_ref[part, :] * (level / total))
                cur[part, :] = now
                after = after + jnp.sum(now, axis=0, keepdims=True)
                low[lax.rem(s + 1, 2), part, :] = now.astype(jnp.bfloat16)
            return after

        lax.fori_loop(0, SRC_STEPS, step, jnp.sum(wide, axis=0, keepdims=True))
        wide = land[:, j].reshape(total, columns).astype(jnp.float32)
        increment = (cur[...] - wide).astype(jnp.bfloat16)
        incs[:, j] = increment.reshape(groups, count, columns)
        back_own(j).start()

        @pl.loop(1, groups)
        def _(i):
            back(j, i, me).start()

        lines[j] = (
            jnp.dot(
                coef_ref[...],
                wide + increment.astype(jnp.float32),
                precision=lax.Precision.HIGHEST,
                preferred_element_type=jnp.float32,
            )
            / total
        )

    filled = [lines[j, 0:3] for j in range(own)]
    filled.append(jnp.zeros((gath.shape[2] - 3 * own, columns), jnp.float32))
    gath[me, band] = jnp.concatenate(filled, axis=0).astype(jnp.bfloat16)

    @pl.loop(1, bands)
    def _(i):
        band_copy(i, band).start()

    @pl.loop(1, bands)
    def _(i):
        band_copy(i, lax.rem(band + bands - i, bands)).wait_recv()

    @pl.loop(1, groups)
    def _(i):
        spread(i, me).start()

    @pl.loop(1, groups)
    def _(i):
        spread(i, from_peer(i)).wait_recv()

    table_ref[...] = gath[...]
    side_copy(0).wait()
    side_copy(1).wait()
    state_ref[...] = hold[...]

    @pl.loop(1, bands)
    def _(i):
        tile_copy(i, band).wait_send()
        band_copy(i, band).wait_send()

    @pl.loop(1, groups)
    def _(i):
        spread(i, me).wait_send()

    @pl.loop(0, own)
    def _(j):
        back_own(j).wait()

        @pl.loop(1, groups)
        def _(i):
            push(j, i, me).wait_send()
            back(j, i, me).wait_send()
            back(j, i, from_peer(i)).wait_recv()


def coupled(sent, quad_matrix, dissipation, coef, both, groups, bands):
    rows, count, columns = sent.shape
    own = rows // groups
    total = groups * count
    held = pl.cdiv(3 * own, 16) * 16
    vmem = pl.BlockSpec(memory_space=pltpu.VMEM)
    anywhere = pl.BlockSpec(memory_space=pl.ANY)
    pair = pltpu.SemaphoreType.DMA((own, groups))
    single = pltpu.SemaphoreType.DMA((own,))
    return pl.pallas_call(
        coupled_kernel,
        in_specs=[anywhere, vmem, vmem, vmem, vmem],
        out_specs=[anywhere, vmem, vmem],
        out_shape=[
            jax.ShapeDtypeStruct(sent.shape, jnp.bfloat16),
            jax.ShapeDtypeStruct((groups, bands, held, columns), jnp.bfloat16),
            jax.ShapeDtypeStruct((3, bands) + both.shape, jnp.float32),
        ],
        scratch_shapes=[
            pltpu.VMEM((groups, own, count, columns), jnp.bfloat16),
            pltpu.VMEM((groups, own, count, columns), jnp.bfloat16),
            pltpu.VMEM((total, columns), jnp.float32),
            pltpu.VMEM((2, total, columns), jnp.bfloat16),
            pltpu.VMEM((own, coef.shape[0], columns), jnp.float32),
            pltpu.VMEM((groups, bands, held, columns), jnp.bfloat16),
            pltpu.VMEM((3, bands) + both.shape, jnp.float32),
            single,
            pair,
            pair,
            single,
            pair,
            pair,
            pltpu.SemaphoreType.DMA((bands,)),
            pltpu.SemaphoreType.DMA((bands,)),
            pltpu.SemaphoreType.DMA((groups,)),
            pltpu.SemaphoreType.DMA((groups,)),
            pltpu.SemaphoreType.DMA((bands,)),
            pltpu.SemaphoreType.DMA((bands,)),
            pltpu.SemaphoreType.DMA((2,)),
            pltpu.SemaphoreType.DMA((2,)),
        ],
        compiler_params=pltpu.CompilerParams(
            collective_id=0, has_side_effects=True, vmem_limit_bytes=VMEM_LIMIT
        ),
    )(sent, quad_matrix, dissipation[:, None], coef, both)


def exchange_sources(sent, quad_matrix, dissipation, coef, groups):
    rows, count, columns = sent.shape
    own = rows // groups
    arrived = lax.all_to_all(sent, "comp", split_axis=0, concat_axis=0, tiled=True)
    base = arrived.reshape(groups, own, count, columns)
    if count % 16:
        base = base.transpose(1, 0, 2, 3).reshape(1, own, groups * count, columns)
    increment, stress = sources(base, quad_matrix, dissipation[:, None], coef)
    if count % 16:
        increment = increment.reshape(own, groups, count, columns).transpose(1, 0, 2, 3)
    returned = lax.all_to_all(
        increment.reshape(rows, count, columns), "comp", split_axis=0, concat_axis=0, tiled=True
    )
    return returned, stress


def on_device(spectrum, wet_mask, quad_matrix, dissipation, circulation, source_points):
    local_count, row_count, columns = spectrum.shape
    groups = lax.axis_size("comp")
    bands = lax.axis_size("band")
    own_rows = row_count // groups
    offset = lax.axis_index("comp") * local_count
    speed_x, speed_y, _ = component_tables(offset, local_count, NF, ND)
    stress_coef = component_tables(0, local_count * groups, NF, ND)[2]
    coef = jnp.pad(stress_coef, ((0, 5), (0, 0)))

    head = spectrum[:, :SUBSTEPS].transpose(1, 0, 2).astype(jnp.bfloat16)
    tail = spectrum[:, row_count - SUBSTEPS :].transpose(1, 0, 2).astype(jnp.bfloat16)
    ends = jnp.concatenate([head, tail], axis=0)
    wet = wet_mask.astype(jnp.float32)
    wet_ends = jnp.concatenate([wet[:SUBSTEPS], wet[row_count - SUBSTEPS :]], axis=0)
    ends = jnp.concatenate([ends, wet_ends.astype(jnp.bfloat16)[:, None]], axis=1)
    before, after = neighbours(ends, "band", 0, SUBSTEPS)
    wet_before = before[:, local_count].astype(jnp.float32)
    wet_after = after[:, local_count].astype(jnp.float32)
    wet = jnp.concatenate([wet_before, wet, wet_after], axis=0)
    density, sent = propagate(
        spectrum, before, after, wet, jnp.stack([speed_x, speed_y], axis=1)
    )

    tile_rows = circulation.shape[1]
    tile_cols = circulation.shape[2]
    margin = 2 * SW_STEPS + 1
    both = jnp.concatenate([circulation, source_points.astype(jnp.float32)], axis=0)
    if local_count % 16:
        increment, stress = exchange_sources(sent, quad_matrix, dissipation, coef, groups)
        own_stress = stress[:, :3].astype(jnp.bfloat16)
        table = lax.all_gather(own_stress, "comp", axis=0)
        table = lax.all_gather(table, "band", axis=1)
        both = lax.all_gather(both, "band", axis=1, tiled=True)
        left, right = neighbours(both, "comp", 2, margin)
    else:
        increment, table, state = coupled(
            sent, quad_matrix, dissipation, coef, both, groups, bands
        )
        table = table[:, :, : 3 * own_rows]
        state = state.transpose(0, 2, 1, 3, 4).reshape(3, 6, bands * tile_rows, tile_cols)
        left, both, right = state[0, ..., tile_cols - margin :], state[1], state[2, ..., :margin]
    wide = jnp.concatenate([left, both, right], axis=2)
    wide_cols = wide.shape[2]
    padded_cols = pl.cdiv(wide_cols, LANES) * LANES
    index = jnp.pad(wide[3:].astype(jnp.int32), ((0, 0), (0, 0), (0, padded_cols - wide_cols)))
    index = index.reshape(3, bands, tile_rows * padded_cols).transpose(1, 0, 2)
    table = table.reshape(groups, bands, own_rows, 3, columns // LANES, LANES)
    table = table.transpose(1, 3, 0, 2, 4, 5).reshape(bands, 3, -1, LANES)
    cell_stress = pick(table, index).reshape(bands, 3, tile_rows, padded_cols)
    cell_stress = cell_stress.transpose(1, 0, 2, 3).reshape(3, -1, padded_cols)[..., :wide_cols]
    new_spectrum = finish(density, increment)

    global_col = (
        lax.axis_index("comp") * tile_cols - margin + jnp.arange(wide_cols, dtype=jnp.int32)
    )
    inside = ((global_col >= 0) & (global_col < tile_cols * groups)).astype(jnp.float32)[None, :]
    rimmed = jnp.pad(cell_stress * inside, ((0, 0), (1, 1), (1, 1)))
    force_down = -(diff_rows(rimmed[0]) + diff_cols(rimmed[1]))
    force_across = -(diff_rows(rimmed[1]) + diff_cols(rimmed[2]))
    height, flow_down, flow_across = wide[0] * inside, wide[1] * inside, wide[2] * inside
    for repeat in range(SW_STEPS):
        down_ext = jnp.pad(flow_down, 1)
        across_ext = jnp.pad(flow_across, 1)
        height = (height - wave_speed * (diff_rows(down_ext) + diff_cols(across_ext))) * inside
        height_ext = jnp.pad(height, 1)
        flow_down = (
            (1.0 - friction) * flow_down
            - wave_speed * diff_rows(height_ext)
            + forcing_gain * force_down
        ) * inside
        flow_across = (
            (1.0 - friction) * flow_across
            - wave_speed * diff_cols(height_ext)
            + forcing_gain * force_across
        ) * inside
    stacked = jnp.stack([height, flow_down, flow_across])
    row_start = lax.axis_index("band") * tile_rows
    own = lax.dynamic_slice_in_dim(stacked, row_start, tile_rows, 1)
    return (new_spectrum, own[:, :, margin : margin + tile_cols])


def solution(mesh):
    in_specs = (
        P("comp", "band", None),
        P("band", None),
        P(),
        P(),
        P(None, "band", "comp"),
        P(None, "band", "comp"),
    )
    out_specs = (P("comp", "band", None), P(None, "band", "comp"))
    return jax.shard_map(
        on_device, mesh=mesh, in_specs=in_specs, out_specs=out_specs, check_vma=False
    )
```

```python
import functools
import math

import jax
import jax.numpy as jnp
from jax import lax
from jax.experimental import pallas as pl
from jax.experimental.pallas import tpu as pltpu
from jax.sharding import PartitionSpec as P

NF = 36
ND = 32
SUBSTEPS = 4
SRC_STEPS = 4
SW_STEPS = 8
COMP_BLOCK = 16
FINISH_BLOCK = 48
LANES = 128
VMEM_LIMIT = 50 * 1024 * 1024

step_source = 0.1
wave_speed = 0.35
friction = 0.05
forcing_gain = 0.15


def neighbours(cells, axis, dim, width):
    count = lax.axis_size(axis)
    ends = count - 1
    head = lax.slice_in_dim(cells, 0, width, axis=dim)
    tail = lax.slice_in_dim(cells, cells.shape[dim] - width, cells.shape[dim], axis=dim)
    before = lax.ppermute(tail, axis, [(i, i + 1) for i in range(ends)])
    after = lax.ppermute(head, axis, [(i + 1, i) for i in range(ends)])
    return before, after


def component_tables(offset, local_count, freqs, headings):
    indices = offset + jnp.arange(local_count, dtype=jnp.int32)
    frequency = (indices // headings).astype(jnp.float32)
    heading = (indices % headings).astype(jnp.float32)
    heading_angle = 2.0 * math.pi * (heading + 0.5) / headings
    fraction = (frequency + 0.5) / freqs
    group_speed = 0.25 + 0.4 * fraction
    wave_ratio = 0.5 + 0.5 * fraction
    cosine = jnp.cos(heading_angle)
    sine_part = jnp.sin(heading_angle)
    stress_coef = jnp.stack(
        [
            wave_ratio * (1.0 + cosine * cosine) - 0.5,
            wave_ratio * sine_part * cosine,
            wave_ratio * (1.0 + sine_part * sine_part) - 0.5,
        ]
    )
    return (group_speed * cosine, group_speed * sine_part, stress_coef)


def propagate_kernel(rows, *refs):
    x_refs = refs[:-6]
    before_ref, after_ref, wet_ref, speed_ref, dens_ref, sent_ref = refs[-6:]
    columns = dens_ref.shape[2]
    lane = lax.broadcasted_iota(jnp.int32, (8, columns), 1)
    before = before_ref[...].astype(jnp.float32)
    after = after_ref[...].astype(jnp.float32)
    total = rows + 2 * SUBSTEPS
    halves = []
    for c0 in range(0, COMP_BLOCK, 8):
        ax = jnp.broadcast_to(speed_ref[c0 : c0 + 8, 0:1], (8, columns))
        ay = jnp.broadcast_to(speed_ref[c0 : c0 + 8, 1:2], (8, columns))
        keep = 1.0 - jnp.abs(ax) - jnp.abs(ay)
        west, east = jnp.maximum(ax, 0.0), jnp.maximum(-ax, 0.0)
        south = jnp.where(lane > 0, jnp.maximum(ay, 0.0), 0.0)
        north = jnp.where(lane < columns - 1, jnp.maximum(-ay, 0.0), 0.0)
        stages = [dict() for _ in range(SUBSTEPS + 1)]
        halves.append((c0, keep, west, east, south, north, stages))
    for r in range(total + SUBSTEPS):
        for c0, keep, west, east, south, north, stages in halves:
            if r < SUBSTEPS:
                stages[0][r] = before[r, c0 : c0 + 8]
            elif r < SUBSTEPS + rows:
                part = pl.ds(c0 * rows + r - SUBSTEPS, 8, stride=rows)
                stages[0][r] = jnp.concatenate([x_ref[part, :] for x_ref in x_refs], axis=1)
            elif r < total:
                stages[0][r] = after[r - SUBSTEPS - rows, c0 : c0 + 8]
            for s in range(SUBSTEPS, 0, -1):
                q = r - 2 * s
                if q < s or q >= total - s:
                    continue
                old = stages[s - 1]
                middle = old[q]
                value = (
                    keep * middle
                    + west * old[q - 1]
                    + east * old[q + 1]
                    + south * pltpu.roll(middle, 1, 1)
                    + north * pltpu.roll(middle, columns - 1, 1)
                ) * wet_ref[q : q + 1, :]
                stages[s][q] = value
                if s == SUBSTEPS:
                    dens_ref[q - SUBSTEPS, c0 : c0 + 8, :] = value
    sent_ref[...] = dens_ref[...].astype(jnp.bfloat16)


def propagate(spectrum, before, after, wet, speeds):
    count, rows, columns = spectrum.shape
    grid = (pl.cdiv(count, COMP_BLOCK),)
    parts = columns // LANES
    flat = spectrum.reshape(count * rows, columns)
    return pl.pallas_call(
        functools.partial(propagate_kernel, rows),
        grid=grid,
        in_specs=[
            pl.BlockSpec((COMP_BLOCK * rows, LANES), functools.partial(lambda p, i: (i, p), p))
            for p in range(parts)
        ]
        + [
            pl.BlockSpec((SUBSTEPS, COMP_BLOCK, columns), lambda i: (0, i, 0)),
            pl.BlockSpec((SUBSTEPS, COMP_BLOCK, columns), lambda i: (0, i, 0)),
            pl.BlockSpec((rows + 2 * SUBSTEPS, columns), lambda i: (0, 0)),
            pl.BlockSpec((COMP_BLOCK, 2), lambda i: (i, 0)),
        ],
        out_specs=[
            pl.BlockSpec((rows, COMP_BLOCK, columns), lambda i: (0, i, 0)),
            pl.BlockSpec((rows, COMP_BLOCK, columns), lambda i: (0, i, 0)),
        ],
        out_shape=[
            jax.ShapeDtypeStruct((rows, count, columns), jnp.float32),
            jax.ShapeDtypeStruct((rows, count, columns), jnp.bfloat16),
        ],
        compiler_params=pltpu.CompilerParams(vmem_limit_bytes=VMEM_LIMIT),
    )(*[flat] * parts, before, after, wet, speeds)


def finish_kernel(rows, dens_ref, inc_ref, out_ref, *parts):
    for r in range(rows):
        value = dens_ref[r] + inc_ref[r].astype(jnp.float32)
        for c0 in range(0, dens_ref.shape[1], 8):
            for p, part in enumerate(parts):
                part[pl.ds(c0 * rows + r, 8, stride=rows), :] = value[
                    c0 : c0 + 8, p * LANES : (p + 1) * LANES
                ]
    for p, part in enumerate(parts):
        out_ref[:, p * LANES : (p + 1) * LANES] = part[...]


def finish(density, increment):
    rows, count, columns = density.shape
    block = COMP_BLOCK if count % FINISH_BLOCK else FINISH_BLOCK
    spec = pl.BlockSpec((rows, block, columns), lambda i: (0, i, 0))
    out = pl.pallas_call(
        functools.partial(finish_kernel, rows),
        grid=(pl.cdiv(count, block),),
        in_specs=[spec, spec],
        out_specs=pl.BlockSpec((block * rows, columns), lambda i: (i, 0)),
        out_shape=jax.ShapeDtypeStruct((count * rows, columns), jnp.float32),
        scratch_shapes=[pltpu.VMEM((block * rows, LANES), jnp.float32)] * (columns // LANES),
        compiler_params=pltpu.CompilerParams(vmem_limit_bytes=VMEM_LIMIT),
    )(density, increment)
    return out.reshape(count, rows, columns)


def row_sources(base_ref, quad_ref, diss_ref, coef_ref, cur, low, inc_ref):
    blocks, count, columns = base_ref.shape
    total = blocks * count
    tiles = 3
    tile = total // tiles
    base = base_ref[...].reshape(total, columns)
    low[0] = base
    cur[...] = base.astype(jnp.float32)
    level = jnp.sum(cur[...], axis=0, keepdims=True)
    for s in range(SRC_STEPS):
        after = jnp.zeros_like(level)
        for t in range(tiles):
            part = slice(t * tile, (t + 1) * tile)
            product = jnp.dot(quad_ref[part, :], low[s % 2], preferred_element_type=jnp.float32)
            now = cur[part, :]
            now = now + step_source * now * (product - diss_ref[part, :] * (level / total))
            cur[part, :] = now
            after = after + jnp.sum(now, axis=0, keepdims=True)
            if s < SRC_STEPS - 1:
                low[(s + 1) % 2, part, :] = now.astype(jnp.bfloat16)
        level = after
    wide = base_ref[...].reshape(total, columns).astype(jnp.float32)
    increment = (cur[...] - wide).astype(jnp.bfloat16)
    inc_ref[...] = increment.reshape(blocks, count, columns)
    coupled = wide + increment.astype(jnp.float32)
    return (
        jnp.dot(
            coef_ref[...],
            coupled,
            precision=lax.Precision.HIGHEST,
            preferred_element_type=jnp.float32,
        )
        / total
    )


def sources_kernel(base_ref, quad_ref, diss_ref, coef_ref, inc_ref, stress_ref, cur, low):
    stress_ref[0] = row_sources(
        base_ref.at[:, 0], quad_ref, diss_ref, coef_ref, cur, low, inc_ref.at[:, 0]
    )


def sources(base, quad_matrix, dissipation, coef):
    blocks, rows, count, columns = base.shape
    total = blocks * count
    return pl.pallas_call(
        sources_kernel,
        grid=(rows,),
        in_specs=[
            pl.BlockSpec((blocks, 1, count, columns), lambda i: (0, i, 0, 0)),
            pl.BlockSpec((total, total), lambda i: (0, 0)),
            pl.BlockSpec((total, 1), lambda i: (0, 0)),
            pl.BlockSpec(coef.shape, lambda i: (0, 0)),
        ],
        out_specs=[
            pl.BlockSpec((blocks, 1, count, columns), lambda i: (0, i, 0, 0)),
            pl.BlockSpec((1, coef.shape[0], columns), lambda i: (i, 0, 0)),
        ],
        out_shape=[
            jax.ShapeDtypeStruct(base.shape, jnp.bfloat16),
            jax.ShapeDtypeStruct((rows, coef.shape[0], columns), jnp.float32),
        ],
        scratch_shapes=[
            pltpu.VMEM((total, columns), jnp.float32),
            pltpu.VMEM((2, total, columns), jnp.bfloat16),
        ],
        compiler_params=pltpu.CompilerParams(vmem_limit_bytes=VMEM_LIMIT),
    )(base, quad_matrix, dissipation, coef)


def pick_kernel(table_ref, index_ref, out_ref):
    high = table_ref.shape[2]
    cells = index_ref.shape[2]
    table = table_ref[0].reshape(3 * high, LANES)
    result = [jnp.zeros((1, cells), jnp.float32) for _ in range(3)]
    for m, weight in enumerate((0.5, 0.3, 0.2)):
        index = index_ref[0, m : m + 1, :]
        low = index % LANES
        top = index // LANES
        lane_hit = lax.broadcasted_iota(jnp.int32, (LANES, cells), 0) == low
        ones = jnp.where(lane_hit, 1.0, 0.0).astype(jnp.bfloat16)
        spread = jnp.dot(table, ones, preferred_element_type=jnp.float32)
        row_hit = lax.broadcasted_iota(jnp.int32, (high, cells), 0) == top
        for k in range(3):
            part = jnp.where(row_hit, spread[k * high : (k + 1) * high], 0.0)
            result[k] = result[k] + weight * jnp.sum(part, axis=0, keepdims=True)
    out_ref[0] = jnp.concatenate(result, axis=0)


def pick(table, index):
    bands, _, high, _ = table.shape
    cells = index.shape[2]
    return pl.pallas_call(
        pick_kernel,
        grid=(bands,),
        in_specs=[
            pl.BlockSpec((1, 3, high, LANES), lambda b: (b, 0, 0, 0)),
            pl.BlockSpec((1, 3, cells), lambda b: (b, 0, 0)),
        ],
        out_specs=pl.BlockSpec((1, 3, cells), lambda b: (b, 0, 0)),
        out_shape=jax.ShapeDtypeStruct((bands, 3, cells), jnp.float32),
        compiler_params=pltpu.CompilerParams(vmem_limit_bytes=VMEM_LIMIT),
    )(table, index)


def diff_rows(extended):
    return 0.5 * (extended[2:, 1:-1] - extended[:-2, 1:-1])


def diff_cols(extended):
    return 0.5 * (extended[1:-1, 2:] - extended[1:-1, :-2])


def coupled_kernel(
    sent, quad_ref, diss_ref, coef_ref, both_ref, returned, table_ref, state_ref, *scratch
):
    land, incs, cur, low, lines, gath, hold = scratch[:7]
    scratch = scratch[1:]
    local_sem, push_send, push_recv, back_local, back_send, back_recv = scratch[6:12]
    band_send, band_recv, comp_send, comp_recv = scratch[12:16]
    tile_send, tile_recv, side_send, side_recv = scratch[16:]
    groups, own, count, columns = land.shape
    total = groups * count
    bands = gath.shape[1]
    me = lax.axis_index("comp")
    band = lax.axis_index("band")

    def comp_copy(src, dst, send, recv, peer):
        return pltpu.make_async_remote_copy(
            src_ref=src,
            dst_ref=dst,
            send_sem=send,
            recv_sem=recv,
            device_id=(peer, band),
            device_id_type=pl.DeviceIdType.MESH,
        )

    def band_copy(i, slot):
        return pltpu.make_async_remote_copy(
            src_ref=gath.at[me, band],
            dst_ref=gath.at[me, slot],
            send_sem=band_send.at[i],
            recv_sem=band_recv.at[i],
            device_id=(me, lax.rem(band + i, bands)),
            device_id_type=pl.DeviceIdType.MESH,
        )

    def to_peer(i):
        return lax.rem(me + i, groups)

    def from_peer(i):
        return lax.rem(me + groups - i, groups)

    def push(j, i, slot):
        peer = to_peer(i)
        return comp_copy(
            sent.at[peer * own + j], land.at[slot, j], push_send.at[j, i], push_recv.at[j, i], peer
        )

    def back(j, i, slot):
        peer = to_peer(i)
        return comp_copy(
            incs.at[peer, j],
            returned.at[slot * own + j],
            back_send.at[j, i],
            back_recv.at[j, i],
            peer,
        )

    def spread(i, slot):
        return comp_copy(gath.at[me], gath.at[slot], comp_send.at[i], comp_recv.at[i], to_peer(i))

    def tile_copy(i, slot):
        return pltpu.make_async_remote_copy(
            src_ref=hold.at[1, band],
            dst_ref=hold.at[1, slot],
            send_sem=tile_send.at[i],
            recv_sem=tile_recv.at[i],
            device_id=(me, lax.rem(band + i, bands)),
            device_id_type=pl.DeviceIdType.MESH,
        )

    def side_copy(k):
        peer = to_peer(1) if k == 0 else from_peer(1)
        return comp_copy(
            hold.at[1], hold.at[2 * k], side_send.at[k], side_recv.at[k], peer
        )

    def push_local(j):
        return pltpu.make_async_copy(sent.at[me * own + j], land.at[me, j], local_sem.at[j])

    def back_own(j):
        return pltpu.make_async_copy(incs.at[me, j], returned.at[me * own + j], back_local.at[j])

    barrier = pltpu.get_barrier_semaphore()

    @pl.loop(1, groups)
    def _(i):
        pl.semaphore_signal(
            barrier, inc=1, device_id=(to_peer(i), band), device_id_type=pl.DeviceIdType.MESH
        )

    @pl.loop(1, bands)
    def _(i):
        pl.semaphore_signal(
            barrier,
            inc=1,
            device_id=(me, lax.rem(band + i, bands)),
            device_id_type=pl.DeviceIdType.MESH,
        )

    pl.semaphore_wait(barrier, groups + bands - 2)

    hold[1, band] = both_ref[...]

    @pl.loop(1, bands)
    def _(i):
        tile_copy(i, band).start()

    @pl.loop(0, own)
    def _(j):
        push_local(j).start()

        @pl.loop(1, groups)
        def _(i):
            push(j, i, me).start()

    @pl.loop(1, bands)
    def _(i):
        tile_copy(i, lax.rem(band + bands - i, bands)).wait_recv()

    side_copy(0).start()
    side_copy(1).start()

    tiles = 3
    tile = total // tiles

    @pl.loop(0, own)
    def _(j):
        push_local(j).wait()

        @pl.loop(1, groups)
        def _(i):
            push(j, i, from_peer(i)).wait_recv()

        base = land[:, j].reshape(total, columns)
        low[0] = base
        wide = base.astype(jnp.float32)
        cur[...] = wide

        def step(s, level):
            after = jnp.zeros_like(level)
            for t in range(tiles):
                part = slice(t * tile, (t + 1) * tile)
                product = jnp.dot(
                    quad_ref[part, :], low[lax.rem(s, 2)], preferred_element_type=jnp.float32
                )
                now = cur[part, :]
                now = now + step_source * now * (product - diss_ref[part, :] * (level / total))
                cur[part, :] = now
                after = after + jnp.sum(now, axis=0, keepdims=True)
                low[lax.rem(s + 1, 2), part, :] = now.astype(jnp.bfloat16)
            return after

        lax.fori_loop(0, SRC_STEPS, step, jnp.sum(wide, axis=0, keepdims=True))
        wide = land[:, j].reshape(total, columns).astype(jnp.float32)
        increment = (cur[...] - wide).astype(jnp.bfloat16)
        incs[:, j] = increment.reshape(groups, count, columns)
        back_own(j).start()

        @pl.loop(1, groups)
        def _(i):
            back(j, i, me).start()

        lines[j] = (
            jnp.dot(
                coef_ref[...],
                wide + increment.astype(jnp.float32),
                precision=lax.Precision.HIGHEST,
                preferred_element_type=jnp.float32,
            )
            / total
        )

    filled = [lines[j, 0:3] for j in range(own)]
    filled.append(jnp.zeros((gath.shape[2] - 3 * own, columns), jnp.float32))
    gath[me, band] = jnp.concatenate(filled, axis=0).astype(jnp.bfloat16)

    @pl.loop(1, bands)
    def _(i):
        band_copy(i, band).start()

    @pl.loop(1, bands)
    def _(i):
        band_copy(i, lax.rem(band + bands - i, bands)).wait_recv()

    @pl.loop(1, groups)
    def _(i):
        spread(i, me).start()

    @pl.loop(1, groups)
    def _(i):
        spread(i, from_peer(i)).wait_recv()

    table_ref[...] = gath[...]
    side_copy(0).wait()
    side_copy(1).wait()
    state_ref[...] = hold[...]

    @pl.loop(1, bands)
    def _(i):
        tile_copy(i, band).wait_send()
        band_copy(i, band).wait_send()

    @pl.loop(1, groups)
    def _(i):
        spread(i, me).wait_send()

    @pl.loop(0, own)
    def _(j):
        back_own(j).wait()

        @pl.loop(1, groups)
        def _(i):
            push(j, i, me).wait_send()
            back(j, i, me).wait_send()
            back(j, i, from_peer(i)).wait_recv()


def coupled(sent, quad_matrix, dissipation, coef, both, groups, bands):
    rows, count, columns = sent.shape
    own = rows // groups
    total = groups * count
    held = pl.cdiv(3 * own, 16) * 16
    vmem = pl.BlockSpec(memory_space=pltpu.VMEM)
    anywhere = pl.BlockSpec(memory_space=pl.ANY)
    pair = pltpu.SemaphoreType.DMA((own, groups))
    single = pltpu.SemaphoreType.DMA((own,))
    return pl.pallas_call(
        coupled_kernel,
        in_specs=[anywhere, vmem, vmem, vmem, vmem],
        out_specs=[anywhere, vmem, vmem],
        out_shape=[
            jax.ShapeDtypeStruct(sent.shape, jnp.bfloat16),
            jax.ShapeDtypeStruct((groups, bands, held, columns), jnp.bfloat16),
            jax.ShapeDtypeStruct((3, bands) + both.shape, jnp.float32),
        ],
        scratch_shapes=[
            pltpu.VMEM((groups, own, count, columns), jnp.bfloat16),
            pltpu.VMEM((groups, own, count, columns), jnp.bfloat16),
            pltpu.VMEM((total, columns), jnp.float32),
            pltpu.VMEM((2, total, columns), jnp.bfloat16),
            pltpu.VMEM((own, coef.shape[0], columns), jnp.float32),
            pltpu.VMEM((groups, bands, held, columns), jnp.bfloat16),
            pltpu.VMEM((3, bands) + both.shape, jnp.float32),
            single,
            pair,
            pair,
            single,
            pair,
            pair,
            pltpu.SemaphoreType.DMA((bands,)),
            pltpu.SemaphoreType.DMA((bands,)),
            pltpu.SemaphoreType.DMA((groups,)),
            pltpu.SemaphoreType.DMA((groups,)),
            pltpu.SemaphoreType.DMA((bands,)),
            pltpu.SemaphoreType.DMA((bands,)),
            pltpu.SemaphoreType.DMA((2,)),
            pltpu.SemaphoreType.DMA((2,)),
        ],
        compiler_params=pltpu.CompilerParams(
            collective_id=0, has_side_effects=True, vmem_limit_bytes=VMEM_LIMIT
        ),
    )(sent, quad_matrix, dissipation[:, None], coef, both)


def exchange_sources(sent, quad_matrix, dissipation, coef, groups):
    rows, count, columns = sent.shape
    own = rows // groups
    arrived = lax.all_to_all(sent, "comp", split_axis=0, concat_axis=0, tiled=True)
    base = arrived.reshape(groups, own, count, columns)
    if count % 16:
        base = base.transpose(1, 0, 2, 3).reshape(1, own, groups * count, columns)
    increment, stress = sources(base, quad_matrix, dissipation[:, None], coef)
    if count % 16:
        increment = increment.reshape(own, groups, count, columns).transpose(1, 0, 2, 3)
    returned = lax.all_to_all(
        increment.reshape(rows, count, columns), "comp", split_axis=0, concat_axis=0, tiled=True
    )
    return returned, stress


def on_device(spectrum, wet_mask, quad_matrix, dissipation, circulation, source_points):
    local_count, row_count, columns = spectrum.shape
    groups = lax.axis_size("comp")
    bands = lax.axis_size("band")
    own_rows = row_count // groups
    offset = lax.axis_index("comp") * local_count
    speed_x, speed_y, _ = component_tables(offset, local_count, NF, ND)
    stress_coef = component_tables(0, local_count * groups, NF, ND)[2]
    coef = jnp.pad(stress_coef, ((0, 5), (0, 0)))

    head = spectrum[:, :SUBSTEPS].transpose(1, 0, 2).astype(jnp.bfloat16)
    tail = spectrum[:, row_count - SUBSTEPS :].transpose(1, 0, 2).astype(jnp.bfloat16)
    ends = jnp.concatenate([head, tail], axis=0)
    wet = wet_mask.astype(jnp.float32)
    wet_ends = jnp.concatenate([wet[:SUBSTEPS], wet[row_count - SUBSTEPS :]], axis=0)
    ends = jnp.concatenate([ends, wet_ends.astype(jnp.bfloat16)[:, None]], axis=1)
    before, after = neighbours(ends, "band", 0, SUBSTEPS)
    wet_before = before[:, local_count].astype(jnp.float32)
    wet_after = after[:, local_count].astype(jnp.float32)
    wet = jnp.concatenate([wet_before, wet, wet_after], axis=0)
    density, sent = propagate(
        spectrum, before, after, wet, jnp.stack([speed_x, speed_y], axis=1)
    )

    tile_rows = circulation.shape[1]
    tile_cols = circulation.shape[2]
    margin = 2 * SW_STEPS + 1
    both = jnp.concatenate([circulation, source_points.astype(jnp.float32)], axis=0)
    if local_count % 16:
        increment, stress = exchange_sources(sent, quad_matrix, dissipation, coef, groups)
        own_stress = stress[:, :3].astype(jnp.bfloat16)
        table = lax.all_gather(own_stress, "comp", axis=0)
        table = lax.all_gather(table, "band", axis=1)
        both = lax.all_gather(both, "band", axis=1, tiled=True)
        left, right = neighbours(both, "comp", 2, margin)
    else:
        increment, table, state = coupled(
            sent, quad_matrix, dissipation, coef, both, groups, bands
        )
        table = table[:, :, : 3 * own_rows]
        state = state.transpose(0, 2, 1, 3, 4).reshape(3, 6, bands * tile_rows, tile_cols)
        left, both, right = state[0, ..., tile_cols - margin :], state[1], state[2, ..., :margin]
    wide = jnp.concatenate([left, both, right], axis=2)
    wide_cols = wide.shape[2]
    padded_cols = pl.cdiv(wide_cols, LANES) * LANES
    index = jnp.pad(wide[3:].astype(jnp.int32), ((0, 0), (0, 0), (0, padded_cols - wide_cols)))
    index = index.reshape(3, bands, tile_rows * padded_cols).transpose(1, 0, 2)
    table = table.reshape(groups, bands, own_rows, 3, columns // LANES, LANES)
    table = table.transpose(1, 3, 0, 2, 4, 5).reshape(bands, 3, -1, LANES)
    cell_stress = pick(table, index).reshape(bands, 3, tile_rows, padded_cols)
    cell_stress = cell_stress.transpose(1, 0, 2, 3).reshape(3, -1, padded_cols)[..., :wide_cols]
    new_spectrum = finish(density, increment)

    global_col = (
        lax.axis_index("comp") * tile_cols - margin + jnp.arange(wide_cols, dtype=jnp.int32)
    )
    inside = ((global_col >= 0) & (global_col < tile_cols * groups)).astype(jnp.float32)[None, :]
    rimmed = jnp.pad(cell_stress * inside, ((0, 0), (1, 1), (1, 1)))
    force_down = -(diff_rows(rimmed[0]) + diff_cols(rimmed[1]))
    force_across = -(diff_rows(rimmed[1]) + diff_cols(rimmed[2]))
    height, flow_down, flow_across = wide[0] * inside, wide[1] * inside, wide[2] * inside
    for repeat in range(SW_STEPS):
        down_ext = jnp.pad(flow_down, 1)
        across_ext = jnp.pad(flow_across, 1)
        height = (height - wave_speed * (diff_rows(down_ext) + diff_cols(across_ext))) * inside
        height_ext = jnp.pad(height, 1)
        flow_down = (
            (1.0 - friction) * flow_down
            - wave_speed * diff_rows(height_ext)
            + forcing_gain * force_down
        ) * inside
        flow_across = (
            (1.0 - friction) * flow_across
            - wave_speed * diff_cols(height_ext)
            + forcing_gain * force_across
        ) * inside
    stacked = jnp.stack([height, flow_down, flow_across])
    row_start = lax.axis_index("band") * tile_rows
    own = lax.dynamic_slice_in_dim(stacked, row_start, tile_rows, 1)
    return (new_spectrum, own[:, :, margin : margin + tile_cols])


def solution(mesh):
    in_specs = (
        P("comp", "band", None),
        P("band", None),
        P(),
        P(),
        P(None, "band", "comp"),
        P(None, "band", "comp"),
    )
    out_specs = (P("comp", "band", None), P(None, "band", "comp"))
    return jax.shard_map(
        on_device, mesh=mesh, in_specs=in_specs, out_specs=out_specs, check_vma=False
    )
```
